512 devices in a mesh: outer: 4 (over y_lo, core), dp: 128 (over z, x, y_hi).
Axes of the slice: x: 4, y: 4 (y_hi: 2, y_lo: 2; y = y_hi * 2 + y_lo), z: 16, core: 2. Of those that a mesh axis runs over, the one named last changes fastest.
Arguments:
- frame_encodings: bfloat16 [16384, 1280], P('dp'), may hold values from -6 to 6
- frame_projector_matrix: bfloat16 [1280, 1024], replicated, may hold values from -0.15625 to 0.15625
- sound_latents: bfloat16 [16384, 1024], P(('outer', 'dp')), may hold values from -0.1875 to 0.1875
- matched_targets: int32 [16384, 5], P('dp'), may hold values from -1 to 16383, as said below
- score_coldness: float32 [1], replicated, may hold values from 30 to 100
- score_offset: float32 [1], replicated, may hold values from -4 to -1
Outputs:
- weight_grad: float32 [1280, 1024], P('outer', 'dp')
The draws below stay inside these ranges and needn't reach their ends.
Inputs may be any that keep to these rules, and one draw needn't show every extreme that they name: `matched_targets`: clips are cut 16 to a recording in time order and placed on rows by a random permutation; a video row's partners are the rows of the clips of its recording at most 2 places from it, itself included, each listed once, the other entries -1. The relation is symmetric. Some row has 5 partners.
All inputs are finite; a program needn't handle non-finite values.
Results may differ from the reference program's by a relative error of at most 0.0034.
Values may be sent and summed in bfloat16 or wider, within the bound.
No kernel may reach another device: no remote copies, remote signals or barrier semaphores. Data moves between devices by JAX's collectives and lax.ppermute only.
A program may use at most 64 MiB of HBM per device.

```python
import jax
import jax.numpy as jnp
from jax import lax

E = 1280
LATENT_DIM = 1024
ROWS_DEV = 128
REACH = 2
TAKES = 16
PARTNERS = 5
SEGMENT_COUNT = 16384


def draw_matched_targets(key, part):
    key = jax.random.fold_in(key, 11)
    slot_of = jax.random.permutation(key, SEGMENT_COUNT).astype(jnp.int32)
    clip_ids = jnp.arange(SEGMENT_COUNT, dtype=jnp.int32)
    place = clip_ids % TAKES
    near = jnp.arange(-REACH, REACH + 1, dtype=jnp.int32)
    moved = place[:, None] + near[None, :]
    inside = (moved >= 0) & (moved < TAKES)
    other_clip = jnp.clip(clip_ids[:, None] + near[None, :], 0, SEGMENT_COUNT - 1)
    listed = jnp.where(inside, slot_of[other_clip], -1).astype(jnp.int32)
    return jnp.zeros((SEGMENT_COUNT, PARTNERS), jnp.int32).at[slot_of].set(listed)


def steps_of(rng, dims, pieces, smallest, top_value):
    gain = 1.0
    for axis_at, shards_of in pieces:
        heights = jax.random.uniform(jax.random.fold_in(jax.random.fold_in(rng, 6), axis_at), (shards_of,), jnp.float32, smallest / len(pieces), top_value / len(pieces))
        gain = gain * jnp.repeat(jnp.exp(heights), dims[axis_at] // shards_of).reshape((-1,) + (1,) * (len(dims) - 1 - axis_at))
    return gain


def gaussian(key, shape, scale, limit, cuts=(), kind=jnp.bfloat16):
    gain = steps_of(key, shape, cuts, -0.22, 0.18) if cuts else 1.0
    entries = jax.random.normal(key, shape, jnp.float32) * scale * gain
    return jnp.minimum(jnp.maximum(entries, -limit), limit).astype(kind)


def setup_inputs(seed: int = 0) -> dict:
    keys = jax.random.split(jax.random.key(seed), 7)
    frame_encodings = gaussian(keys[0], (SEGMENT_COUNT, E), 1.0, 6.0, ((0, 128),))
    frame_projector_matrix = gaussian(keys[1], (E, LATENT_DIM), E ** -0.5, 0.15625)
    sound_latents = gaussian(keys[2], (SEGMENT_COUNT, LATENT_DIM), LATENT_DIM ** -0.5, 0.1875, ((0, 512),))
    matched_targets = draw_matched_targets(jax.random.fold_in(keys[6], 71), 0)
    score_coldness = jnp.clip(jax.random.uniform(keys[4], (1,), jnp.float32, 30.0, 100.0), 30.0, 100.0)
    score_offset = jnp.clip(jax.random.uniform(keys[5], (1,), jnp.float32, -4.0, -1.0), -4.0, -1.0)
    return {"frame_encodings": frame_encodings, "frame_projector_matrix": frame_projector_matrix, "sound_latents": sound_latents, "matched_targets": matched_targets, "score_coldness": score_coldness, "score_offset": score_offset}


def reference(frame_encodings, frame_projector_matrix, sound_latents, matched_targets, score_coldness, score_offset):
    sharpness_factor = score_coldness[0]
    offset_adjusted = score_offset[0]
    projected = jnp.dot(frame_encodings, frame_projector_matrix, preferred_element_type=jnp.float32)
    magnitude = jnp.sqrt(lax.optimization_barrier(jnp.sum(projected * projected, axis=1, keepdims=True)) + 1e-06)
    unit = projected / magnitude
    unit_b = unit.astype(jnp.bfloat16)
    column_ids = jnp.arange(SEGMENT_COUNT, dtype=jnp.int32)

    def one_block(inputs):
        unit_length_latents, partner_rows = inputs
        similarity_scores = sharpness_factor * lax.dot_general(unit_length_latents, sound_latents, (((1,), (1,)), ((), ())), preferred_element_type=jnp.float32) + offset_adjusted
        positive = jnp.any(partner_rows[:, :, None] == column_ids[None, None, :], axis=1).astype(jnp.float32)
        pair_weight = (jax.nn.sigmoid(similarity_scores) - positive).astype(jnp.bfloat16)
        return jnp.dot(pair_weight, sound_latents, preferred_element_type=jnp.float32)
    blocks = SEGMENT_COUNT // ROWS_DEV
    accumulated_contributions = lax.map(one_block, (unit_b.reshape(blocks, ROWS_DEV, LATENT_DIM), matched_targets.reshape(blocks, ROWS_DEV, PARTNERS)))
    latent_derivative = sharpness_factor * accumulated_contributions.reshape(SEGMENT_COUNT, LATENT_DIM)
    inner = lax.optimization_barrier(jnp.sum(unit * latent_derivative, axis=1, keepdims=True))
    grad_proj = ((latent_derivative - unit * inner) / magnitude).astype(jnp.bfloat16)
    return lax.dot_general(frame_encodings, grad_proj, (((0,), (0,)), ((), ())), preferred_element_type=jnp.float32)
```

```python
import functools

import jax
import jax.numpy as jnp
from jax import lax
from jax.experimental import pallas as pl
from jax.experimental.pallas import tpu as pltpu
from jax.sharding import Mesh, PartitionSpec as P

BF = jnp.bfloat16
F32 = jnp.float32
AXES = ("ylo", "core", "z", "x", "yhi")
SIZES = (2, 2, 16, 4, 2)
DP = ("z", "x", "yhi")
PLANE = ("x", "yhi", "ylo")
LINE = ("z", "ylo", "core")
PAD = 128
CompilerParams = pltpu.CompilerParams


def project_kernel(x_ref, w_ref, unit_ref, unit_b_ref, mag_ref):
    e = w_ref.shape[0]
    projected = jnp.dot(x_ref[:, :e], w_ref[...], preferred_element_type=F32)
    mag = jnp.sqrt(jnp.sum(projected * projected, axis=1, keepdims=True) + 1e-06)
    unit = projected / mag
    unit_ref[...] = unit
    unit_b_ref[...] = unit.astype(BF)
    mag_ref[...] = jnp.broadcast_to(mag, mag_ref.shape)


def pair_kernel(place_ref, scale_ref, unit_ref, unit_b_ref, mag_ref, t_ref, own_ref, other_ref, out_ref):
    cold = scale_ref[0]
    offset = scale_ref[1]
    unit_b = unit_b_ref[...]
    targets = t_ref[...].astype(F32)
    total = None
    for side, audio_ref in enumerate((own_ref, other_ref)):
        audio = audio_ref[...]
        n = audio.shape[0]
        lane = lax.broadcasted_iota(jnp.int32, (1, n), 1)
        ids = (place_ref[side] + (lane // 32) * 256 + lane % 32).astype(F32)
        sims = lax.dot_general(unit_b, audio, (((1,), (1,)), ((), ())), preferred_element_type=F32)
        logits = cold * sims + offset
        hit = None
        for p in range(5):
            target = targets[:, 2 * p : 2 * p + 1] * 128.0 + targets[:, 2 * p + 1 : 2 * p + 2]
            same = target == ids
            hit = same if hit is None else hit | same
        weight = (jax.nn.sigmoid(logits) - jnp.where(hit, 1.0, 0.0)).astype(BF)
        term = jnp.dot(weight, audio, preferred_element_type=F32)
        total = term if total is None else total + term
    grad = cold * total
    unit = unit_ref[...]
    inner = jnp.sum(unit * grad, axis=1, keepdims=True)
    gp = ((grad - unit * inner) / mag_ref[:, :1]).astype(BF)
    for t in range(8):
        out_ref[t, 0] = gp[:, 128 * t : 128 * (t + 1)]


def weight_kernel(place_ref, g_ref, x_ref, out_ref):
    total = g_ref[0].astype(F32)
    for s in range(1, g_ref.shape[0]):
        total = total + g_ref[s].astype(F32)
    gp = total.astype(BF)
    rows = x_ref[pl.ds(pl.multiple_of(place_ref[2] * 256, 256), 256), :1280]
    part = lax.dot_general(gp, rows, (((0,), (0,)), ((), ())), preferred_element_type=F32)
    for o in range(4):
        out_ref[:, o] = part[:, 320 * o : 320 * (o + 1)].reshape(16, 8, 320)


def by_owner(a):
    n = a.shape[0]
    return a.reshape(n, 16, 8, 8).transpose(0, 2, 1, 3).reshape(n, 1024)


def local(frames, projector, sounds, matched, coldness, offset):
    ylo, core, z, x, yhi = (lax.axis_index(a) for a in AXES)
    mine = by_owner(sounds)
    own = lax.all_to_all(
        jnp.broadcast_to(mine[None], (16, 32, 1024)), "z", 0, 0, tiled=True
    ).reshape(512, 1024)
    other = lax.ppermute(own, "core", [(0, 1), (1, 0)])
    base = ylo * 8192 + (2 * x + yhi) * 32
    place = jnp.stack([base + core * 4096, base + (1 - core) * 4096, ylo]).astype(jnp.int32)

    halves = jnp.stack([matched >> 7, matched & 127], axis=2).reshape(128, 10).astype(BF)
    wide = jnp.concatenate([frames, jnp.pad(halves, ((0, 0), (0, PAD - 10)))], axis=1)
    wide = lax.dynamic_slice_in_dim(wide, core * 64, 64, 0)
    row = lax.all_gather(wide, "x", axis=0, tiled=True)
    far = lax.ppermute(row, "yhi", [(0, 1), (1, 0)])
    rows = jnp.concatenate([jnp.where(yhi == 0, row, far), jnp.where(yhi == 0, far, row)], axis=0)

    width = 1280 + PAD
    block = 128
    unit, unit_b, mag = pl.pallas_call(
        project_kernel,
        grid=(4,),
        in_specs=[
            pl.BlockSpec((block, width), lambda i: (i, 0)),
            pl.BlockSpec((1280, 1024), lambda i: (0, 0)),
        ],
        out_specs=[
            pl.BlockSpec((block, 1024), lambda i: (i, 0)),
            pl.BlockSpec((block, 1024), lambda i: (i, 0)),
            pl.BlockSpec((block, 128), lambda i: (i, 0)),
        ],
        out_shape=[
            jax.ShapeDtypeStruct((512, 1024), F32),
            jax.ShapeDtypeStruct((512, 1024), BF),
            jax.ShapeDtypeStruct((512, 128), F32),
        ],
        compiler_params=CompilerParams(vmem_limit_bytes=40 * 2**20),
        cost_estimate=pl.CostEstimate(flops=2 * 512 * 1280 * 1024, bytes_accessed=8 * 2**20, transcendentals=0),
    )(rows, by_owner(projector))

    scale = jnp.concatenate([coldness, offset])
    smem = pl.BlockSpec(memory_space=pltpu.SMEM)
    parts = pl.pallas_call(
        pair_kernel,
        grid=(4,),
        in_specs=[
            smem,
            smem,
            pl.BlockSpec((block, 1024), lambda i: (i, 0)),
            pl.BlockSpec((block, 1024), lambda i: (i, 0)),
            pl.BlockSpec((block, 128), lambda i: (i, 0)),
            pl.BlockSpec((block, PAD), lambda i: (i, 10)),
            pl.BlockSpec((512, 1024), lambda i: (0, 0)),
            pl.BlockSpec((512, 1024), lambda i: (0, 0)),
        ],
        out_specs=pl.BlockSpec((8, 1, block, 128), lambda i: (0, i // 2, i % 2, 0)),
        out_shape=jax.ShapeDtypeStruct((8, 2, 256, 128), BF),
        compiler_params=CompilerParams(vmem_limit_bytes=40 * 2**20),
        cost_estimate=pl.CostEstimate(flops=4 * 512 * 1024 * 1024, bytes_accessed=8 * 2**20, transcendentals=2**20),
    )(place, scale, unit, unit_b, mag, rows, own, other)

    terms = lax.all_to_all(parts.reshape(16, 256, 128), PLANE, 0, 0, tiled=True)
    vmem = pl.BlockSpec(memory_space=pltpu.VMEM)
    pieces = pl.pallas_call(
        weight_kernel,
        in_specs=[smem, vmem, vmem],
        out_specs=vmem,
        out_shape=jax.ShapeDtypeStruct((16, 4, 8, 320), F32),
        compiler_params=CompilerParams(vmem_limit_bytes=40 * 2**20),
    )(place, terms, rows)
    sums = lax.all_to_all(pieces.reshape(64, 8, 320), LINE, 0, 0, tiled=True)
    return jnp.sum(sums, axis=0).T


def solution(mesh):
    fine = Mesh(mesh.devices.reshape(SIZES), AXES)
    return jax.shard_map(
        local,
        mesh=fine,
        in_specs=(P(DP, None), P(), P(AXES, None), P(DP, None), P(), P()),
        out_specs=P(("ylo", "core"), DP),
        check_vma=False,
    )
```

```python
import jax
import jax.numpy as jnp
from jax import lax
from jax.experimental import pallas as pl
from jax.experimental.pallas import tpu as pltpu
from jax.sharding import Mesh, PartitionSpec as P

BF = jnp.bfloat16
F32 = jnp.float32
AXES = ("ylo", "core", "z", "x", "yhi")
SIZES = (2, 2, 16, 4, 2)
DP = ("z", "x", "yhi")
PLANE = ("x", "yhi", "ylo")
LINE = ("core", "z")
PAD = 128
CompilerParams = pltpu.CompilerParams


def project_kernel(x_ref, w_ref, unit_ref, unit_b_ref, mag_ref, order_ref):
    n = order_ref.shape[0]
    was = lax.broadcasted_iota(jnp.int32, (n, 1024), 0) + pl.program_id(0) * n
    goes = (was // 8 % 8) * 128 + (was // 64) * 8 + was % 8
    lane = lax.broadcasted_iota(jnp.int32, (n, 1024), 1)
    order_ref[...] = jnp.where(goes == lane, 1.0, 0.0).astype(BF)
    e = w_ref.shape[0]
    projected = jnp.dot(x_ref[:, :e], w_ref[...], preferred_element_type=F32)
    mag = jnp.sqrt(jnp.sum(projected * projected, axis=1, keepdims=True) + 1e-06)
    unit = projected / mag
    unit_ref[...] = unit
    unit_b_ref[...] = unit.astype(BF)
    mag_ref[...] = jnp.broadcast_to(mag, mag_ref.shape)


def pair_kernel(scale_ref, unit_ref, unit_b_ref, mag_ref, t_ref, ids_ref, order_ref, *refs):
    *audio_refs, out_ref = refs
    cold = scale_ref[0]
    offset = scale_ref[1]
    unit_b = unit_b_ref[...]
    targets = t_ref[...].astype(F32)
    total = None
    at = 0
    for audio_ref in audio_refs:
        audio = audio_ref[...]
        n = audio.shape[0]
        ids = ids_ref[:1, at : at + n]
        at += n
        sims = lax.dot_general(unit_b, audio, (((1,), (1,)), ((), ())), preferred_element_type=F32)
        logits = cold * sims + offset
        hit = None
        for p in range(5):
            target = targets[:, 2 * p : 2 * p + 1] * 128.0 + targets[:, 2 * p + 1 : 2 * p + 2]
            same = target == ids
            hit = same if hit is None else hit | same
        weight = (jax.nn.sigmoid(logits) - jnp.where(hit, 1.0, 0.0)).astype(BF)
        term = jnp.dot(weight, audio, preferred_element_type=F32)
        total = term if total is None else total + term
    grad = cold * total
    unit = unit_ref[...]
    inner = jnp.sum(unit * grad, axis=1, keepdims=True)
    gp = ((grad - unit * inner) / mag_ref[:, :1]).astype(BF)
    gp = jnp.dot(gp, order_ref[...], preferred_element_type=F32).astype(BF)
    for t in range(8):
        out_ref[t, 0] = gp[:, 128 * t : 128 * (t + 1)]


def sum_kernel(g_ref, out_ref):
    total = g_ref[0].astype(F32)
    for s in range(1, g_ref.shape[0]):
        total = total + g_ref[s].astype(F32)
    out_ref[...] = total.astype(BF)


def weight_kernel(place_ref, g_ref, far_ref, x_ref, out_ref):
    ylo = place_ref[0]
    lanes = pl.ds(pl.multiple_of(ylo * 640, 128), 640)
    part = None
    for ref, half in ((g_ref, ylo), (far_ref, 1 - ylo)):
        rows = x_ref[pl.ds(pl.multiple_of(half * 256, 256), 256), lanes]
        term = lax.dot_general(ref[...], rows, (((0,), (0,)), ((), ())), preferred_element_type=F32)
        part = term if part is None else part + term
    for c in range(2):
        out_ref[c] = part[:, 320 * c : 320 * (c + 1)].reshape(16, 8, 320).astype(out_ref.dtype)


def fetch(a, far):
    perm = []
    for z in range(16):
        perm.append(((z + far) % 16, z))
        perm.append((16 + (z - far) % 16, 16 + z))
    return lax.ppermute(a, ("core", "z"), perm)


def swap(a, axis):
    return lax.ppermute(a, axis, [(0, 1), (1, 0)])


def local(frames, projector, sounds, matched, coldness, offset):
    ylo, core, z, x, yhi = (lax.axis_index(a) for a in AXES)
    up6 = fetch(sounds, 6)
    down6 = fetch(sounds, -6)
    up2 = fetch(jnp.concatenate([sounds, up6, down6], axis=0), 2)
    down2 = fetch(jnp.concatenate([sounds, up6], axis=0), -2)
    fours = jnp.concatenate([sounds, up2[32:], down2[32:]], axis=0)
    twos = jnp.concatenate([up6, down6, up2[:32], down2[:32]], axis=0)
    up1 = fetch(fours, 1)
    down1 = fetch(fours, -1)
    even = jnp.concatenate([fours, twos], axis=0)
    odd = jnp.concatenate([up1, down1], axis=0)
    far_even = swap(even, "core")
    far_odd = swap(odd, "core")
    evens = jnp.array([0, 8, -4, 4, 6, -6, 2, -2], jnp.int32)
    odds = jnp.array([1, 9, -3, 5, -1, 7, -5, 3], jnp.int32)
    sign = 1 - 2 * core
    steps = jnp.concatenate([sign * evens, -sign * evens, sign * odds, -sign * odds])
    cores = jnp.concatenate([jnp.full(8, core), jnp.full(8, 1 - core)] * 2)
    blocks = ylo * 8192 + cores * 4096 + (z + steps) % 16 * 256 + (2 * x + yhi) * 32
    ids = (blocks[:, None] + jnp.arange(32)[None, :]).reshape(1, 1024).astype(F32)
    ids = jnp.broadcast_to(ids, (8, 1024))

    halves = jnp.stack([matched >> 7, matched & 127], axis=2).reshape(128, 10).astype(BF)
    wide = jnp.concatenate([frames, jnp.pad(halves, ((0, 0), (0, PAD - 10)))], axis=1)
    wide = lax.dynamic_slice_in_dim(wide, core * 64, 64, 0)
    row = lax.all_gather(wide, "x", axis=0, tiled=True)
    far = swap(row, "yhi")
    rows = jnp.concatenate([jnp.where(yhi == 0, row, far), jnp.where(yhi == 0, far, row)], axis=0)

    width = 1280 + PAD
    block = 128
    whole = lambda i: (0, 0)
    by_row = lambda i: (i, 0)
    unit, unit_b, mag, order = pl.pallas_call(
        project_kernel,
        grid=(4,),
        in_specs=[pl.BlockSpec((block, width), by_row), pl.BlockSpec((1280, 1024), whole)],
        out_specs=[
            pl.BlockSpec((block, 1024), by_row),
            pl.BlockSpec((block, 1024), by_row),
            pl.BlockSpec((block, 128), by_row),
            pl.BlockSpec((256, 1024), by_row),
        ],
        out_shape=[
            jax.ShapeDtypeStruct((512, 1024), F32),
            jax.ShapeDtypeStruct((512, 1024), BF),
            jax.ShapeDtypeStruct((512, 128), F32),
            jax.ShapeDtypeStruct((1024, 1024), BF),
        ],
        compiler_params=CompilerParams(vmem_limit_bytes=40 * 2**20),
        cost_estimate=pl.CostEstimate(flops=2 * 512 * 1280 * 1024, bytes_accessed=8 * 2**20, transcendentals=0),
    )(rows, projector)

    scale = jnp.concatenate([coldness, offset])
    smem = pl.BlockSpec(memory_space=pltpu.SMEM)
    vmem = pl.BlockSpec(memory_space=pltpu.VMEM)
    parts = pl.pallas_call(
        pair_kernel,
        grid=(4,),
        in_specs=[
            smem,
            pl.BlockSpec((block, 1024), by_row),
            pl.BlockSpec((block, 1024), by_row),
            pl.BlockSpec((block, 128), by_row),
            pl.BlockSpec((block, PAD), lambda i: (i, 10)),
            pl.BlockSpec((8, 1024), whole),
            pl.BlockSpec((1024, 1024), whole),
        ]
        + [pl.BlockSpec((256, 1024), whole)] * 4,
        out_specs=pl.BlockSpec((8, 1, block, 128), lambda i: (0, i // 2, i % 2, 0)),
        out_shape=jax.ShapeDtypeStruct((8, 2, 256, 128), BF),
        compiler_params=CompilerParams(vmem_limit_bytes=40 * 2**20),
        cost_estimate=pl.CostEstimate(flops=5 * 512 * 1024 * 1024, bytes_accessed=8 * 2**20, transcendentals=2**20),
    )(scale, unit, unit_b, mag, rows, ids, order, even, far_even, odd, far_odd)

    terms = lax.all_to_all(parts.reshape(16, 256, 128), PLANE, 0, 0, tiled=True)
    params = CompilerParams(vmem_limit_bytes=40 * 2**20)
    gp = pl.pallas_call(
        sum_kernel, in_specs=[vmem], out_specs=vmem, out_shape=jax.ShapeDtypeStruct((256, 128), BF), compiler_params=params
    )(terms)
    far_gp = swap(gp, "ylo")
    pieces = pl.pallas_call(
        weight_kernel,
        in_specs=[smem, vmem, vmem, vmem],
        out_specs=vmem,
        out_shape=jax.ShapeDtypeStruct((2, 16, 8, 320), BF),
        compiler_params=params,
    )(ylo.reshape(1).astype(jnp.int32), gp, far_gp, rows)
    sums = lax.all_to_all(pieces.reshape(32, 8, 320), LINE, 0, 0, tiled=True)
    return jnp.sum(sums.astype(F32), axis=0).T


def solution(mesh):
    fine = Mesh(mesh.devices.reshape(SIZES), AXES)
    return jax.shard_map(
        local,
        mesh=fine,
        in_specs=(P(DP, None), P(), P(AXES, None), P(DP, None), P(), P()),
        out_specs=P(("ylo", "core"), DP),
        check_vma=False,
    )
```

```python
import jax
import jax.numpy as jnp
import numpy as np
from jax import lax
from jax.experimental import pallas as pl
from jax.experimental.pallas import tpu as pltpu
from jax.sharding import Mesh, PartitionSpec as P

BF = jnp.bfloat16
F32 = jnp.float32
AXES = ("ylo", "core", "zp", "par", "x", "yhi")
SIZES = (2, 2, 8, 2, 4, 2)
DP = ("zp", "par", "x", "yhi")
Z = ("zp", "par")
PLANE = ("x", "yhi", "ylo")
CHIP = ("ylo", "core")
PAD = 128
PARAMS = pltpu.CompilerParams(vmem_limit_bytes=24 * 2**20)


def column_order():
    was = np.arange(1024)
    goes = (was // 8 % 8) * 128 + (was // 64) * 8 + was % 8
    return jnp.asarray(goes[:, None] == was[None, :], BF)


def project_kernel(x_ref, w_ref, unit_ref, unit_b_ref, mag_ref, t_ref):
    projected = jnp.dot(x_ref[:, : w_ref.shape[0]], w_ref[...], preferred_element_type=F32)
    mag = jnp.sqrt(jnp.sum(projected * projected, axis=1, keepdims=True) + 1e-06)
    unit = projected / mag
    unit_ref[...] = unit
    unit_b_ref[...] = unit.astype(BF)
    mag_ref[...] = jnp.broadcast_to(mag, mag_ref.shape)
    t_ref[...] = x_ref[:, w_ref.shape[0] :]


def pair_kernel(scale_ref, place_ref, *refs):
    video, ids_ref, order_ref, audio_refs, out_ref = refs[:8], refs[8], refs[9], refs[10:14], refs[14]
    unit, unit_b, mag, x = (jnp.concatenate([a[...], b[...]], axis=0) for a, b in zip(video[:4], video[4:]))
    cold = scale_ref[0]
    offset = scale_ref[1]
    halves = x.astype(F32)
    targets = [halves[:, 2 * p : 2 * p + 1] * 128.0 + halves[:, 2 * p + 1 : 2 * p + 2] for p in range(5)]
    total = None
    at = 0
    for audio_ref in audio_refs:
        audio = audio_ref[...]
        n = audio.shape[0]
        ids = ids_ref[:1, at : at + n]
        at += n
        sims = lax.dot_general(unit_b, audio, (((1,), (1,)), ((), ())), preferred_element_type=F32)
        logits = cold * sims + offset
        hit = None
        for target in targets:
            same = target == ids
            hit = same if hit is None else hit | same
        weight = (jax.nn.sigmoid(logits) - jnp.where(hit, 1.0, 0.0)).astype(BF)
        term = jnp.dot(weight, audio, preferred_element_type=F32)
        total = term if total is None else total + term
    grad = cold * total
    inner = jnp.sum(unit * grad, axis=1, keepdims=True)
    gp = ((grad - unit * inner) / mag[:, :1]).astype(BF)
    gp = jnp.dot(gp, order_ref[...], preferred_element_type=F32).astype(BF)
    for h in range(2):
        half = place_ref[0] if h == 0 else 1 - place_ref[0]
        for t in range(8):
            out_ref[2 * t + half] = gp[256 * h : 256 * (h + 1), 128 * t : 128 * (t + 1)]


def weight_kernel(place_ref, g_ref, row_ref, far_ref, out_ref):
    total = g_ref[0].astype(F32)
    for s in range(1, g_ref.shape[0]):
        total = total + g_ref[s].astype(F32)
    gp = total.astype(BF)
    x = jnp.where(place_ref[1] == 1, row_ref[:, :1280], far_ref[:, :1280])
    part = lax.dot_general(gp, x, (((0,), (0,)), ((), ())), preferred_element_type=F32).astype(BF)
    for o in range(4):
        out_ref[o] = part[:, 320 * o : 320 * (o + 1)].reshape(16, 8, 320)


def add_kernel(in_ref, out_ref):
    total = in_ref[0].astype(F32)
    for s in range(1, in_ref.shape[0]):
        total = total + in_ref[s].astype(F32)
    out_ref[...] = total.astype(out_ref.dtype)


def fetch(a, far):
    return lax.ppermute(a, Z, [((z + far) % 16, z) for z in range(16)])


def swap(a, axis):
    return lax.ppermute(a, axis, [(0, 1), (1, 0)])


def local(frames, projector, sounds, matched, coldness, offset):
    ylo, core, zp, par, x, yhi = (lax.axis_index(a) for a in AXES)
    smem = pl.BlockSpec(memory_space=pltpu.SMEM)
    vmem = pl.BlockSpec(memory_space=pltpu.VMEM)

    same = lax.all_to_all(jnp.broadcast_to(sounds[None], (8, 32, 1024)), "zp", 0, 0, tiled=True).reshape(256, 1024)

    halves = jnp.stack([matched >> 7, matched & 127], axis=2).reshape(128, 10).astype(BF)
    wide = jnp.concatenate([frames, jnp.pad(halves, ((0, 0), (0, PAD - 10)))], axis=1)
    wide = lax.dynamic_slice_in_dim(wide, core * 64, 64, 0)
    row = lax.all_gather(wide, "x", axis=0, tiled=True)
    same, _ = lax.optimization_barrier((same, row))
    far = swap(row, "yhi")

    other = jnp.concatenate([fetch(same[:128], 1), fetch(same[128:], -1)], axis=0)
    far_same = swap(same, "core")
    far_other = swap(other, "core")
    place = jnp.stack([yhi, 1 - (yhi ^ ylo)]).astype(jnp.int32)
    pars = jnp.stack([par, par, 1 - par, 1 - par])
    cores = jnp.stack([core, 1 - core, core, 1 - core])
    firsts = ylo * 8192 + cores * 4096 + pars * 256 + (2 * x + yhi) * 32
    inside = np.arange(8)[:, None] * 512 + np.arange(32)[None, :]
    ids = (firsts[:, None] + jnp.asarray(inside.reshape(1, 256), jnp.int32)).astype(F32).reshape(1, 1024)

    project = pl.pallas_call(
        project_kernel,
        in_specs=[vmem, vmem],
        out_specs=[vmem] * 4,
        out_shape=[
            jax.ShapeDtypeStruct((256, 1024), F32),
            jax.ShapeDtypeStruct((256, 1024), BF),
            jax.ShapeDtypeStruct((256, 128), F32),
            jax.ShapeDtypeStruct((256, PAD), BF),
        ],
        compiler_params=PARAMS,
        cost_estimate=pl.CostEstimate(flops=2 * 256 * 1280 * 1024, bytes_accessed=5 * 2**20, transcendentals=0),
    )
    video = [*project(row, projector), *project(far, projector)]
    parts = pl.pallas_call(
        pair_kernel,
        in_specs=[smem, smem] + [vmem] * 14,
        out_specs=vmem,
        out_shape=jax.ShapeDtypeStruct((16, 256, 128), BF),
        compiler_params=PARAMS,
        cost_estimate=pl.CostEstimate(flops=5 * 512 * 1024 * 1024, bytes_accessed=8 * 2**20, transcendentals=2**20),
    )(
        jnp.concatenate([coldness, offset]),
        place,
        *video,
        ids,
        column_order(),
        same,
        far_same,
        other,
        far_other,
    )

    terms = lax.all_to_all(parts, PLANE, 0, 0, tiled=True)
    pieces = pl.pallas_call(
        weight_kernel,
        in_specs=[smem, vmem, vmem, vmem],
        out_specs=vmem,
        out_shape=jax.ShapeDtypeStruct((4, 16, 8, 320), BF),
        compiler_params=PARAMS,
    )(place, terms, row, far)
    mine = lax.all_to_all(pieces, CHIP, 0, 0, tiled=True)
    mine = pl.pallas_call(
        add_kernel, in_specs=[vmem], out_specs=vmem, out_shape=jax.ShapeDtypeStruct((16, 8, 320), BF), compiler_params=PARAMS
    )(mine)
    sums = lax.all_to_all(mine, Z, 0, 0, tiled=True)
    return jnp.sum(sums.astype(F32), axis=0).T


def solution(mesh):
    fine = Mesh(mesh.devices.reshape(SIZES), AXES)
    return jax.shard_map(
        local,
        mesh=fine,
        in_specs=(P(DP, None), P(), P(AXES, None), P(DP, None), P(), P()),
        out_specs=P(CHIP, DP),
        check_vma=False,
    )
```

```python
import jax
import jax.numpy as jnp
import numpy as np
from jax import lax
from jax.experimental import pallas as pl
from jax.experimental.pallas import tpu as pltpu
from jax.sharding import Mesh, PartitionSpec as P

BF = jnp.bfloat16
F32 = jnp.float32
AXES = ("ylo", "core", "zp", "par", "x", "yhi")
SIZES = (2, 2, 8, 2, 4, 2)
DP = ("zp", "par", "x", "yhi")
Z = ("zp", "par")
PLANE = ("x", "yhi", "ylo")
CHIP = ("ylo", "core")
PAD = 128
PARAMS = pltpu.CompilerParams(vmem_limit_bytes=24 * 2**20)


def column_order():
    was = np.arange(1024)
    goes = (was // 8 % 8) * 128 + (was // 64) * 8 + was % 8
    return jnp.asarray(goes[:, None] == was[None, :], BF)


def project_kernel(x_ref, w_ref, unit_ref, unit_b_ref, mag_ref, t_ref):
    projected = jnp.dot(x_ref[:, : w_ref.shape[0]], w_ref[...], preferred_element_type=F32)
    mag = jnp.sqrt(jnp.sum(projected * projected, axis=1, keepdims=True) + 1e-06)
    unit = projected / mag
    unit_ref[...] = unit
    unit_b_ref[...] = unit.astype(BF)
    mag_ref[...] = jnp.broadcast_to(mag, mag_ref.shape)
    t_ref[...] = x_ref[:, w_ref.shape[0] :]


def pair_kernel(scale_ref, place_ref, *refs):
    video, ids_ref, order_ref, audio_refs, out_ref = refs[:8], refs[8], refs[9], refs[10:14], refs[14]
    unit, unit_b, mag, x = (jnp.concatenate([a[...], b[...]], axis=0) for a, b in zip(video[:4], video[4:]))
    cold = scale_ref[0]
    offset = scale_ref[1]
    halves = x.astype(F32)
    targets = [halves[:, 2 * p : 2 * p + 1] * 128.0 + halves[:, 2 * p + 1 : 2 * p + 2] for p in range(5)]
    total = None
    at = 0
    for audio_ref in audio_refs:
        audio = audio_ref[...]
        n = audio.shape[0]
        ids = ids_ref[:1, at : at + n]
        at += n
        sims = lax.dot_general(unit_b, audio, (((1,), (1,)), ((), ())), preferred_element_type=F32)
        logits = cold * sims + offset
        hit = None
        for target in targets:
            same = target == ids
            hit = same if hit is None else hit | same
        weight = (jax.nn.sigmoid(logits) - jnp.where(hit, 1.0, 0.0)).astype(BF)
        term = jnp.dot(weight, audio, preferred_element_type=F32)
        total = term if total is None else total + term
    grad = cold * total
    inner = jnp.sum(unit * grad, axis=1, keepdims=True)
    gp = ((grad - unit * inner) / mag[:, :1]).astype(BF)
    gp = jnp.dot(gp, order_ref[...], preferred_element_type=F32).astype(BF)
    for h in range(2):
        half = place_ref[0] if h == 0 else 1 - place_ref[0]
        for t in range(8):
            out_ref[2 * t + half] = gp[256 * h : 256 * (h + 1), 128 * t : 128 * (t + 1)]


def sum_kernel(g_ref, out_ref):
    total = g_ref[0].astype(F32)
    for s in range(1, g_ref.shape[0]):
        total = total + g_ref[s].astype(F32)
    out_ref[...] = total.astype(BF)


def weight_kernel(place_ref, mine_ref, other_ref, row_ref, far_ref, keep_ref, give_ref):
    lanes = pl.ds(pl.multiple_of(place_ref[2] * 640, 128), 640)
    mine, other = mine_ref[...], other_ref[...]
    own = place_ref[1] == 1
    part = None
    for gp, rows in ((jnp.where(own, mine, other), row_ref[:, lanes]), (jnp.where(own, other, mine), far_ref[:, lanes])):
        term = lax.dot_general(gp, rows, (((0,), (0,)), ((), ())), preferred_element_type=F32)
        part = term if part is None else part + term
    first, second = (part[:, 320 * c : 320 * (c + 1)].reshape(16, 8, 320) for c in range(2))
    core = place_ref[3]
    keep_ref[...] = jnp.where(core == 0, first, second)
    give_ref[...] = jnp.where(core == 0, second, first).astype(BF)


def add_kernel(a_ref, b_ref, out_ref):
    out_ref[...] = (a_ref[...] + b_ref[...].astype(F32)).astype(BF)


def fetch(a):
    perm = [((z + 1) % 16, z) for z in range(16)] + [(16 + (z - 1) % 16, 16 + z) for z in range(16)]
    return lax.ppermute(a, ("core", "zp", "par"), perm)


def swap(a, axis):
    return lax.ppermute(a, axis, [(0, 1), (1, 0)])


def local(frames, projector, sounds, matched, coldness, offset):
    ylo, core, zp, par, x, yhi = (lax.axis_index(a) for a in AXES)
    smem = pl.BlockSpec(memory_space=pltpu.SMEM)
    vmem = pl.BlockSpec(memory_space=pltpu.VMEM)

    same = lax.all_to_all(jnp.broadcast_to(sounds[None], (8, 32, 1024)), "zp", 0, 0, tiled=True).reshape(256, 1024)

    halves = jnp.stack([matched >> 7, matched & 127], axis=2).reshape(128, 10).astype(BF)
    wide = jnp.concatenate([frames, jnp.pad(halves, ((0, 0), (0, PAD - 10)))], axis=1)
    wide = lax.dynamic_slice_in_dim(wide, core * 64, 64, 0)
    across = lax.ppermute(wide, ("ylo", "yhi"), [(0, 3), (3, 0), (1, 2), (2, 1)])
    row = lax.all_gather(wide, "x", axis=0, tiled=True)
    far = lax.all_gather(across, "x", axis=0, tiled=True)
    same, _, _ = lax.optimization_barrier((same, row, far))

    other = fetch(same)
    far_same = swap(same, "core")
    far_other = swap(other, "core")
    place = jnp.stack([yhi, 1 - (yhi ^ ylo), ylo, core]).astype(jnp.int32)
    pars = jnp.stack([par, par, 1 - par, 1 - par])
    cores = jnp.stack([core, 1 - core, core, 1 - core])
    firsts = ylo * 8192 + cores * 4096 + pars * 256 + (2 * x + yhi) * 32
    inside = np.arange(8)[:, None] * 512 + np.arange(32)[None, :]
    ids = (firsts[:, None] + jnp.asarray(inside.reshape(1, 256), jnp.int32)).astype(F32).reshape(1, 1024)

    project = pl.pallas_call(
        project_kernel,
        in_specs=[vmem, vmem],
        out_specs=[vmem] * 4,
        out_shape=[
            jax.ShapeDtypeStruct((256, 1024), F32),
            jax.ShapeDtypeStruct((256, 1024), BF),
            jax.ShapeDtypeStruct((256, 128), F32),
            jax.ShapeDtypeStruct((256, PAD), BF),
        ],
        compiler_params=PARAMS,
        cost_estimate=pl.CostEstimate(flops=2 * 256 * 1280 * 1024, bytes_accessed=5 * 2**20, transcendentals=0),
    )
    video = [*project(row, projector), *project(far, projector)]
    parts = pl.pallas_call(
        pair_kernel,
        in_specs=[smem, smem] + [vmem] * 14,
        out_specs=vmem,
        out_shape=jax.ShapeDtypeStruct((16, 256, 128), BF),
        compiler_params=PARAMS,
        cost_estimate=pl.CostEstimate(flops=5 * 512 * 1024 * 1024, bytes_accessed=8 * 2**20, transcendentals=2**20),
    )(
        jnp.concatenate([coldness, offset]),
        place,
        *video,
        ids,
        column_order(),
        same,
        far_same,
        other,
        far_other,
    )

    terms = lax.all_to_all(parts, PLANE, 0, 0, tiled=True)
    mine = pl.pallas_call(
        sum_kernel, in_specs=[vmem], out_specs=vmem, out_shape=jax.ShapeDtypeStruct((256, 128), BF), compiler_params=PARAMS
    )(terms)
    keep, give = pl.pallas_call(
        weight_kernel,
        in_specs=[smem] + [vmem] * 4,
        out_specs=[vmem, vmem],
        out_shape=[jax.ShapeDtypeStruct((16, 8, 320), F32), jax.ShapeDtypeStruct((16, 8, 320), BF)],
        compiler_params=PARAMS,
    )(place, mine, swap(mine, "ylo"), row, far)
    mine = pl.pallas_call(
        add_kernel,
        in_specs=[vmem, vmem],
        out_specs=vmem,
        out_shape=jax.ShapeDtypeStruct((16, 8, 320), BF),
        compiler_params=PARAMS,
    )(keep, swap(give, "core"))
    sums = lax.all_to_all(mine, Z, 0, 0, tiled=True)
    return jnp.sum(sums.astype(F32), axis=0).T


def solution(mesh):
    fine = Mesh(mesh.devices.reshape(SIZES), AXES)
    return jax.shard_map(
        local,
        mesh=fine,
        in_specs=(P(DP, None), P(), P(AXES, None), P(DP, None), P(), P()),
        out_specs=P(CHIP, DP),
        check_vma=False,
    )
```

```python
import jax
import jax.numpy as jnp
import numpy as np
from jax import lax
from jax.experimental import pallas as pl
from jax.experimental.pallas import tpu as pltpu
from jax.sharding import Mesh, PartitionSpec as P

BF = jnp.bfloat16
F32 = jnp.float32
AXES = ("ylo", "core", "zp", "par", "x", "yhi")
SIZES = (2, 2, 8, 2, 4, 2)
DP = ("zp", "par", "x", "yhi")
Z = ("zp", "par")
PLANE = ("x", "yhi", "ylo")
CHIP = ("ylo", "core")
PAD = 128
PARAMS = pltpu.CompilerParams(vmem_limit_bytes=18 * 2**20)


def column_order():
    was = np.arange(1024)
    goes = (was // 8 % 8) * 128 + (was // 64) * 8 + was % 8
    return jnp.asarray(goes[:, None] == was[None, :], BF)


def project_kernel(place_ref, own_ref, next_ref, across_ref, last_ref, w_ref, x_ref, t_ref, unit_ref, unit_b_ref, mag_ref):
    e = w_ref.shape[0]
    x, yhi = place_ref[4], place_ref[0]
    for k, ref in enumerate((own_ref, next_ref, across_ref, last_ref)):
        for h in range(2):
            half = yhi if h == 0 else 1 - yhi
            at = pl.ds(pl.multiple_of(lax.rem(x + k, 4) * 128 + half * 64, 64), 64)
            x_ref[at, :] = ref[64 * h : 64 * (h + 1), :e]
            t_ref[at, :] = ref[64 * h : 64 * (h + 1), e:]
    projected = jnp.dot(x_ref[...], w_ref[...], preferred_element_type=F32)
    mag = jnp.sqrt(jnp.sum(projected * projected, axis=1, keepdims=True) + 1e-06)
    unit = projected / mag
    unit_ref[...] = unit
    unit_b_ref[...] = unit.astype(BF)
    mag_ref[...] = jnp.broadcast_to(mag, mag_ref.shape)


def pair_kernel(scale_ref, t_ref, unit_ref, unit_b_ref, mag_ref, ids_ref, order_ref, *refs):
    *audio_refs, out_ref = refs
    cold = scale_ref[0]
    offset = scale_ref[1]
    unit_b = unit_b_ref[...]
    halves = t_ref[...].astype(F32)
    targets = [halves[:, 2 * p : 2 * p + 1] * 128.0 + halves[:, 2 * p + 1 : 2 * p + 2] for p in range(5)]
    total = None
    at = 0
    for audio_ref in audio_refs:
        audio = audio_ref[...]
        n = audio.shape[0]
        ids = ids_ref[:1, at : at + n]
        at += n
        sims = lax.dot_general(unit_b, audio, (((1,), (1,)), ((), ())), preferred_element_type=F32)
        logits = cold * sims + offset
        hit = None
        for target in targets:
            same = target == ids
            hit = same if hit is None else hit | same
        weight = (jax.nn.sigmoid(logits) - jnp.where(hit, 1.0, 0.0)).astype(BF)
        term = jnp.dot(weight, audio, preferred_element_type=F32)
        total = term if total is None else total + term
    grad = cold * total
    unit = unit_ref[...]
    inner = jnp.sum(unit * grad, axis=1, keepdims=True)
    gp = ((grad - unit * inner) / mag_ref[:, :1]).astype(BF)
    gp = jnp.dot(gp, order_ref[...], preferred_element_type=F32).astype(BF)
    for h in range(2):
        for t in range(8):
            out_ref[2 * t + h] = gp[256 * h : 256 * (h + 1), 128 * t : 128 * (t + 1)]


def sum_kernel(g_ref, out_ref):
    total = g_ref[0].astype(F32)
    for s in range(1, g_ref.shape[0]):
        total = total + g_ref[s].astype(F32)
    out_ref[...] = total.astype(BF)


def weight_kernel(place_ref, mine_ref, other_ref, x_ref, keep_ref, give_ref):
    ylo = place_ref[2]
    lanes = pl.ds(pl.multiple_of(ylo * 640, 128), 640)
    part = None
    for gp_ref, half in ((mine_ref, ylo), (other_ref, 1 - ylo)):
        rows = x_ref[pl.ds(pl.multiple_of(half * 256, 256), 256), lanes]
        term = lax.dot_general(gp_ref[...], rows, (((0,), (0,)), ((), ())), preferred_element_type=F32)
        part = term if part is None else part + term
    first, second = (part[:, 320 * c : 320 * (c + 1)].reshape(16, 8, 320) for c in range(2))
    core = place_ref[3]
    keep_ref[...] = jnp.where(core == 0, first, second)
    give_ref[...] = jnp.where(core == 0, second, first).astype(BF)


def add_kernel(a_ref, b_ref, out_ref):
    out_ref[...] = (a_ref[...] + b_ref[...].astype(F32)).astype(BF)


def fetch(a):
    perm = [((z + 1) % 16, z) for z in range(16)] + [(16 + (z - 1) % 16, 16 + z) for z in range(16)]
    return lax.ppermute(a, ("core", "zp", "par"), perm)


def after(a, *others):
    anywhere = pl.BlockSpec(memory_space=pl.ANY)
    return pl.pallas_call(
        lambda *refs: None,
        in_specs=[anywhere] * (1 + len(others)),
        out_specs=anywhere,
        out_shape=jax.ShapeDtypeStruct(a.shape, a.dtype),
        input_output_aliases={0: 0},
        compiler_params=pltpu.CompilerParams(vmem_limit_bytes=2**16),
    )(a, *others)


def swap(a, axis):
    return lax.ppermute(a, axis, [(0, 1), (1, 0)])


def local(frames, projector, sounds, matched, coldness, offset):
    ylo, core, zp, par, x, yhi = (lax.axis_index(a) for a in AXES)
    smem = pl.BlockSpec(memory_space=pltpu.SMEM)
    vmem = pl.BlockSpec(memory_space=pltpu.VMEM)

    same = lax.all_to_all(jnp.broadcast_to(sounds[None], (8, 32, 1024)), "zp", 0, 0, tiled=True).reshape(256, 1024)

    halves = jnp.stack([matched >> 7, matched & 127], axis=2).reshape(128, 10).astype(BF)
    wide = jnp.concatenate([frames, jnp.pad(halves, ((0, 0), (0, PAD - 10)))], axis=1)
    wide = lax.dynamic_slice_in_dim(wide, core * 64, 64, 0)
    across = lax.ppermute(wide, ("ylo", "yhi"), [(0, 3), (3, 0), (1, 2), (2, 1)])
    wide = jnp.concatenate([wide, across], axis=0)
    turned = [lax.ppermute(wide, "x", [((i + k) % 4, i) for i in range(4)]) for k in (1, 2, 3)]
    same = after(same, *turned)

    other = fetch(same)
    far_same = swap(same, "core")
    place = jnp.stack([yhi, yhi, ylo, core, x]).astype(jnp.int32)
    pars = jnp.stack([par, par, 1 - par, 1 - par])
    cores = jnp.stack([core, 1 - core, core, 1 - core])
    firsts = ylo * 8192 + cores * 4096 + pars * 256 + (2 * x + yhi) * 32
    inside = np.arange(8)[:, None] * 512 + np.arange(32)[None, :]
    ids = (firsts[:, None] + jnp.asarray(inside.reshape(1, 256), jnp.int32)).astype(F32).reshape(1, 1024)

    rows, *video = pl.pallas_call(
        project_kernel,
        in_specs=[smem] + [vmem] * 5,
        out_specs=[vmem] * 5,
        out_shape=[
            jax.ShapeDtypeStruct((512, 1280), BF),
            jax.ShapeDtypeStruct((512, PAD), BF),
            jax.ShapeDtypeStruct((512, 1024), F32),
            jax.ShapeDtypeStruct((512, 1024), BF),
            jax.ShapeDtypeStruct((512, 128), F32),
        ],
        compiler_params=PARAMS,
        cost_estimate=pl.CostEstimate(flops=2 * 512 * 1280 * 1024, bytes_accessed=9 * 2**20, transcendentals=0),
    )(place, wide, *turned, projector)
    far_other = swap(other, "core")
    parts = pl.pallas_call(
        pair_kernel,
        in_specs=[smem] + [vmem] * 10,
        out_specs=vmem,
        out_shape=jax.ShapeDtypeStruct((16, 256, 128), BF),
        compiler_params=PARAMS,
        cost_estimate=pl.CostEstimate(flops=5 * 512 * 1024 * 1024, bytes_accessed=8 * 2**20, transcendentals=2**20),
    )(
        jnp.concatenate([coldness, offset]),
        *video,
        ids,
        column_order(),
        same,
        far_same,
        other,
        far_other,
    )

    terms = lax.all_to_all(parts, PLANE, 0, 0, tiled=True)
    mine = pl.pallas_call(
        sum_kernel, in_specs=[vmem], out_specs=vmem, out_shape=jax.ShapeDtypeStruct((256, 128), BF), compiler_params=PARAMS
    )(terms)
    keep, give = pl.pallas_call(
        weight_kernel,
        in_specs=[smem] + [vmem] * 3,
        out_specs=[vmem, vmem],
        out_shape=[jax.ShapeDtypeStruct((16, 8, 320), F32), jax.ShapeDtypeStruct((16, 8, 320), BF)],
        compiler_params=PARAMS,
    )(place, mine, swap(mine, "ylo"), rows)
    mine = pl.pallas_call(
        add_kernel,
        in_specs=[vmem, vmem],
        out_specs=vmem,
        out_shape=jax.ShapeDtypeStruct((16, 8, 320), BF),
        compiler_params=PARAMS,
    )(keep, swap(give, "core"))
    sums = lax.all_to_all(mine, Z, 0, 0, tiled=True)
    return jnp.sum(sums.astype(F32), axis=0).T


def solution(mesh):
    fine = Mesh(mesh.devices.reshape(SIZES), AXES)
    return jax.shard_map(
        local,
        mesh=fine,
        in_specs=(P(DP, None), P(), P(AXES, None), P(DP, None), P(), P()),
        out_specs=P(CHIP, DP),
        check_vma=False,
    )
```

```python
import functools

import jax
import jax.numpy as jnp
import numpy as np
from jax import lax
from jax.experimental import pallas as pl
from jax.experimental.pallas import tpu as pltpu
from jax.sharding import Mesh, PartitionSpec as P

BF = jnp.bfloat16
F32 = jnp.float32
AXES = ("ylo", "core", "z", "x", "yhi")
SIZES = (2, 2, 16, 4, 2)
DP = ("z", "x", "yhi")
PLANE = ("x", "yhi", "ylo")
CHIP = ("ylo", "core")
PAD = 128
PARAMS = pltpu.CompilerParams(vmem_limit_bytes=18 * 2**20)


def column_order():
    was = np.arange(1024)
    goes = (was // 8 % 8) * 128 + (was // 64) * 8 + was % 8
    return jnp.asarray(goes[:, None] == was[None, :], BF)


def project_kernel(place_ref, own_ref, next_ref, across_ref, last_ref, w_ref, x_ref, t_ref, unit_ref, unit_b_ref, mag_ref):
    e = w_ref.shape[0]
    x, yhi = place_ref[3], place_ref[0]
    for k, ref in enumerate((own_ref, next_ref, across_ref, last_ref)):
        for h in range(2):
            half = yhi if h == 0 else 1 - yhi
            at = pl.ds(pl.multiple_of(lax.rem(x + k, 4) * 128 + half * 64, 64), 64)
            x_ref[at, :] = ref[64 * h : 64 * (h + 1), :e]
            t_ref[at, :] = ref[64 * h : 64 * (h + 1), e:]
    projected = jnp.dot(x_ref[...], w_ref[...], preferred_element_type=F32)
    mag = jnp.sqrt(jnp.sum(projected * projected, axis=1, keepdims=True) + 1e-06)
    unit = projected / mag
    unit_ref[...] = unit
    unit_b_ref[...] = unit.astype(BF)
    mag_ref[...] = jnp.broadcast_to(mag, mag_ref.shape)


def pair_kernel(scale_ref, t_ref, unit_ref, unit_b_ref, mag_ref, ids_ref, order_ref, *refs):
    *audio_refs, out_ref = refs
    cold = scale_ref[0]
    offset = scale_ref[1]
    unit_b = unit_b_ref[...]
    halves = t_ref[...].astype(F32)
    targets = [halves[:, 2 * p : 2 * p + 1] * 128.0 + halves[:, 2 * p + 1 : 2 * p + 2] for p in range(5)]
    total = None
    at = 0
    for audio_ref in audio_refs:
        audio = audio_ref[...]
        n = audio.shape[0]
        ids = ids_ref[:1, at : at + n]
        at += n
        sims = lax.dot_general(unit_b, audio, (((1,), (1,)), ((), ())), preferred_element_type=F32)
        logits = cold * sims + offset
        hit = None
        for target in targets:
            same = target == ids
            hit = same if hit is None else hit | same
        weight = (jax.nn.sigmoid(logits) - jnp.where(hit, 1.0, 0.0)).astype(BF)
        term = jnp.dot(weight, audio, preferred_element_type=F32)
        total = term if total is None else total + term
    grad = cold * total
    unit = unit_ref[...]
    inner = jnp.sum(unit * grad, axis=1, keepdims=True)
    gp = ((grad - unit * inner) / mag_ref[:, :1]).astype(BF)
    gp = jnp.dot(gp, order_ref[...], preferred_element_type=F32).astype(BF)
    for h in range(2):
        for t in range(8):
            out_ref[2 * t + h] = gp[256 * h : 256 * (h + 1), 128 * t : 128 * (t + 1)]


def sum_kernel(g_ref, out_ref):
    total = g_ref[0].astype(F32)
    for s in range(1, g_ref.shape[0]):
        total = total + g_ref[s].astype(F32)
    out_ref[...] = total.astype(BF)


def weight_kernel(place_ref, mine_ref, other_ref, x_ref, keep_ref, give_ref):
    ylo = place_ref[1]
    lanes = pl.ds(pl.multiple_of(ylo * 640, 128), 640)
    part = None
    for gp_ref, half in ((mine_ref, ylo), (other_ref, 1 - ylo)):
        rows = x_ref[pl.ds(pl.multiple_of(half * 256, 256), 256), lanes]
        term = lax.dot_general(gp_ref[...], rows, (((0,), (0,)), ((), ())), preferred_element_type=F32)
        part = term if part is None else part + term
    first, second = (part[:, 320 * c : 320 * (c + 1)].reshape(16, 8, 320) for c in range(2))
    core = place_ref[2]
    keep_ref[...] = jnp.where(core == 0, first, second)
    give_ref[...] = jnp.where(core == 0, second, first).astype(BF)


def add_kernel(a_ref, b_ref, out_ref):
    out_ref[...] = (a_ref[...] + b_ref[...].astype(F32)).astype(BF)


def fetch(a, far, axis, n):
    perm = [((i + far) % n, i) for i in range(n)] + [(n + (i - far) % n, n + i) for i in range(n)]
    return lax.ppermute(a, ("core", axis), perm)


def stack_kernel(*refs, takes):
    for out_ref, take in zip(refs[-len(takes) :], takes):
        at = 0
        for i in take:
            n = refs[i].shape[0]
            out_ref[at : at + n] = refs[i][...]
            at += n


def stack(arrays, *takes):
    vmem = pl.BlockSpec(memory_space=pltpu.VMEM)
    return pl.pallas_call(
        functools.partial(stack_kernel, takes=takes),
        in_specs=[vmem] * len(arrays),
        out_specs=[vmem] * len(takes),
        out_shape=[
            jax.ShapeDtypeStruct((sum(arrays[i].shape[0] for i in take), arrays[0].shape[1]), BF) for take in takes
        ],
        compiler_params=pltpu.CompilerParams(vmem_limit_bytes=4 * 2**20),
    )(*arrays)


def swap(a, axis):
    return lax.ppermute(a, axis, [(0, 1), (1, 0)])


def local(frames, projector, sounds, matched, coldness, offset):
    ylo, core, z, x, yhi = (lax.axis_index(a) for a in AXES)
    smem = pl.BlockSpec(memory_space=pltpu.SMEM)
    vmem = pl.BlockSpec(memory_space=pltpu.VMEM)

    up6 = fetch(sounds, 6, "z", 16)
    down6 = fetch(sounds, -6, "z", 16)
    three, two = stack([sounds, up6, down6], (0, 1, 2), (0, 1))
    up2 = fetch(three, 2, "z", 16)
    down2 = fetch(two, -2, "z", 16)
    (even,) = stack([three, up2, down2], (0, 1, 2))
    odd = fetch(even, 1, "z", 16)
    far_even = swap(even, "core")
    far_odd = swap(odd, "core")
    sign = 1 - 2 * core
    evens = jnp.array([0, 6, -6, 2, 8, -4, -2, 4], jnp.int32)
    steps = jnp.stack([sign * evens, -sign * evens, sign * (evens + 1), -sign * (evens + 1)])
    cores = jnp.stack([core, 1 - core, core, 1 - core])
    firsts = ylo * 8192 + cores[:, None] * 4096 + (z + steps) % 16 * 256 + (2 * x + yhi) * 32
    ids = (firsts[:, :, None] + jnp.arange(32, dtype=jnp.int32)).astype(F32).reshape(1, 1024)
    place = jnp.stack([yhi, ylo, core, x]).astype(jnp.int32)

    halves = jnp.stack([matched >> 7, matched & 127], axis=2).reshape(128, 10).astype(BF)
    wide = jnp.concatenate([frames, jnp.pad(halves, ((0, 0), (0, PAD - 10)))], axis=1)
    wide = lax.dynamic_slice_in_dim(wide, core * 64, 64, 0)
    across = lax.ppermute(wide, ("ylo", "yhi"), [(0, 3), (3, 0), (1, 2), (2, 1)])
    wide = jnp.concatenate([wide, across], axis=0)
    after = lax.ppermute(wide, "x", [((i + 1) % 4, i) for i in range(4)])
    before = lax.ppermute(wide, "x", [((i - 1) % 4, i) for i in range(4)])
    opposite = fetch(jnp.where(core == 0, after, before), 1, "x", 4)

    rows, *video = pl.pallas_call(
        project_kernel,
        in_specs=[smem] + [vmem] * 5,
        out_specs=[vmem] * 5,
        out_shape=[
            jax.ShapeDtypeStruct((512, 1280), BF),
            jax.ShapeDtypeStruct((512, PAD), BF),
            jax.ShapeDtypeStruct((512, 1024), F32),
            jax.ShapeDtypeStruct((512, 1024), BF),
            jax.ShapeDtypeStruct((512, 128), F32),
        ],
        compiler_params=PARAMS,
        cost_estimate=pl.CostEstimate(flops=2 * 512 * 1280 * 1024, bytes_accessed=9 * 2**20, transcendentals=0),
    )(place, wide, after, opposite, before, projector)
    parts = pl.pallas_call(
        pair_kernel,
        in_specs=[smem] + [vmem] * 10,
        out_specs=vmem,
        out_shape=jax.ShapeDtypeStruct((16, 256, 128), BF),
        compiler_params=PARAMS,
        cost_estimate=pl.CostEstimate(flops=5 * 512 * 1024 * 1024, bytes_accessed=8 * 2**20, transcendentals=2**20),
    )(
        jnp.concatenate([coldness, offset]),
        *video,
        ids,
        column_order(),
        even,
        far_even,
        odd,
        far_odd,
    )

    terms = lax.all_to_all(parts, PLANE, 0, 0, tiled=True)
    mine = pl.pallas_call(
        sum_kernel, in_specs=[vmem], out_specs=vmem, out_shape=jax.ShapeDtypeStruct((256, 128), BF), compiler_params=PARAMS
    )(terms)
    keep, give = pl.pallas_call(
        weight_kernel,
        in_specs=[smem] + [vmem] * 3,
        out_specs=[vmem, vmem],
        out_shape=[jax.ShapeDtypeStruct((16, 8, 320), F32), jax.ShapeDtypeStruct((16, 8, 320), BF)],
        compiler_params=PARAMS,
    )(place, mine, swap(mine, "ylo"), rows)
    mine = pl.pallas_call(
        add_kernel,
        in_specs=[vmem, vmem],
        out_specs=vmem,
        out_shape=jax.ShapeDtypeStruct((16, 8, 320), BF),
        compiler_params=PARAMS,
    )(keep, swap(give, "core"))
    sums = lax.all_to_all(mine, "z", 0, 0, tiled=True)
    return jnp.sum(sums.astype(F32), axis=0).T


def solution(mesh):
    fine = Mesh(mesh.devices.reshape(SIZES), AXES)
    return jax.shard_map(
        local,
        mesh=fine,
        in_specs=(P(DP, None), P(), P(AXES, None), P(DP, None), P(), P()),
        out_specs=P(CHIP, DP),
        check_vma=False,
    )
```

```python
import jax
import jax.numpy as jnp
import numpy as np
from jax import lax
from jax.experimental import pallas as pl
from jax.experimental.pallas import tpu as pltpu
from jax.sharding import Mesh, PartitionSpec as P

BF = jnp.bfloat16
F32 = jnp.float32
AXES = ("ylo", "core", "zp", "par", "x", "yhi")
SIZES = (2, 2, 8, 2, 4, 2)
DP = ("zp", "par", "x", "yhi")
Z = ("zp", "par")
PLANE = ("x", "yhi", "ylo")
CHIP = ("ylo", "core")
PAD = 128
PARAMS = pltpu.CompilerParams(vmem_limit_bytes=18 * 2**20)


def column_order():
    was = np.arange(1024)
    goes = (was // 8 % 8) * 128 + (was // 64) * 8 + was % 8
    return jnp.asarray(goes[:, None] == was[None, :], BF)


def project_kernel(place_ref, own_ref, next_ref, across_ref, last_ref, w_ref, x_ref, t_ref, unit_ref, unit_b_ref, mag_ref, held, sems):
    e = w_ref.shape[0]
    step = e // 4
    copies = []
    for c in range(4):
        some = pl.ds(c * step, step)
        copies.append(pltpu.make_async_copy(w_ref.at[some], held.at[some], sems.at[c]))
        copies[-1].start()
    x, yhi = place_ref[3], place_ref[0]
    for k, ref in enumerate((own_ref, next_ref, across_ref, last_ref)):
        for h in range(2):
            half = yhi if h == 0 else 1 - yhi
            at = pl.ds(pl.multiple_of(lax.rem(x + k, 4) * 128 + half * 64, 64), 64)
            x_ref[at, :] = ref[64 * h : 64 * (h + 1), :e]
            t_ref[at, :] = ref[64 * h : 64 * (h + 1), e:]
    projected = None
    for c, copy in enumerate(copies):
        copy.wait()
        some = slice(c * step, (c + 1) * step)
        term = jnp.dot(x_ref[:, some], held[some], preferred_element_type=F32)
        projected = term if projected is None else projected + term
    mag = jnp.sqrt(jnp.sum(projected * projected, axis=1, keepdims=True) + 1e-06)
    unit = projected / mag
    unit_ref[...] = unit
    unit_b_ref[...] = unit.astype(BF)
    mag_ref[...] = jnp.broadcast_to(mag, mag_ref.shape)


def pair_kernel(scale_ref, t_ref, unit_ref, unit_b_ref, mag_ref, ids_ref, order_ref, *refs):
    *audio_refs, out_ref = refs
    cold = scale_ref[0]
    offset = scale_ref[1]
    unit_b = unit_b_ref[...]
    halves = t_ref[...].astype(F32)
    targets = [halves[:, 2 * p : 2 * p + 1] * 128.0 + halves[:, 2 * p + 1 : 2 * p + 2] for p in range(5)]
    total = None
    at = 0
    for audio_ref in audio_refs:
        audio = audio_ref[...]
        n = audio.shape[0]
        ids = ids_ref[:1, at : at + n]
        at += n
        sims = lax.dot_general(unit_b, audio, (((1,), (1,)), ((), ())), preferred_element_type=F32)
        logits = cold * sims + offset
        hit = None
        for target in targets:
            same = target == ids
            hit = same if hit is None else hit | same
        weight = (jax.nn.sigmoid(logits) - jnp.where(hit, 1.0, 0.0)).astype(BF)
        term = jnp.dot(weight, audio, preferred_element_type=F32)
        total = term if total is None else total + term
    grad = cold * total
    unit = unit_ref[...]
    inner = jnp.sum(unit * grad, axis=1, keepdims=True)
    gp = ((grad - unit * inner) / mag_ref[:, :1]).astype(BF)
    gp = jnp.dot(gp, order_ref[...], preferred_element_type=F32).astype(BF)
    for h in range(2):
        for t in range(8):
            out_ref[2 * t + h] = gp[256 * h : 256 * (h + 1), 128 * t : 128 * (t + 1)]


def sum_kernel(g_ref, out_ref):
    total = g_ref[0].astype(F32)
    for s in range(1, g_ref.shape[0]):
        total = total + g_ref[s].astype(F32)
    out_ref[...] = total.astype(BF)


def weight_kernel(place_ref, mine_ref, other_ref, x_ref, keep_ref, give_ref):
    ylo = place_ref[1]
    lanes = pl.ds(pl.multiple_of(ylo * 640, 128), 640)
    part = None
    for gp_ref, half in ((mine_ref, ylo), (other_ref, 1 - ylo)):
        rows = x_ref[pl.ds(pl.multiple_of(half * 256, 256), 256), lanes]
        term = lax.dot_general(gp_ref[...], rows, (((0,), (0,)), ((), ())), preferred_element_type=F32)
        part = term if part is None else part + term
    first, second = (part[:, 320 * c : 320 * (c + 1)].reshape(16, 8, 320) for c in range(2))
    core = place_ref[2]
    keep_ref[...] = jnp.where(core == 0, first, second)
    give_ref[...] = jnp.where(core == 0, second, first).astype(BF)


def add_kernel(a_ref, b_ref, out_ref):
    out_ref[...] = (a_ref[...] + b_ref[...].astype(F32)).astype(BF)


def fetch(a, axes, n):
    perm = [((i + 1) % n, i) for i in range(n)] + [(n + (i - 1) % n, n + i) for i in range(n)]
    return lax.ppermute(a, ("core", *axes), perm)


def behind(a, *others):
    anywhere = pl.BlockSpec(memory_space=pl.ANY)
    return pl.pallas_call(
        lambda *refs: None,
        in_specs=[anywhere] * (1 + len(others)),
        out_specs=anywhere,
        out_shape=jax.ShapeDtypeStruct(a.shape, a.dtype),
        input_output_aliases={0: 0},
        compiler_params=pltpu.CompilerParams(vmem_limit_bytes=2**16),
    )(a, *others)


def swap(a, axis):
    return lax.ppermute(a, axis, [(0, 1), (1, 0)])


def local(frames, projector, sounds, matched, coldness, offset):
    ylo, core, zp, par, x, yhi = (lax.axis_index(a) for a in AXES)
    smem = pl.BlockSpec(memory_space=pltpu.SMEM)
    vmem = pl.BlockSpec(memory_space=pltpu.VMEM)

    even = lax.all_to_all(jnp.broadcast_to(sounds[None], (8, 32, 1024)), "zp", 0, 0, tiled=True).reshape(256, 1024)
    pars = jnp.stack([par, par, 1 - par, 1 - par])
    cores = jnp.stack([core, 1 - core, core, 1 - core])
    firsts = ylo * 8192 + cores * 4096 + pars * 256 + (2 * x + yhi) * 32
    inside = np.arange(8)[:, None] * 512 + np.arange(32)[None, :]
    ids = (firsts[:, None] + jnp.asarray(inside.reshape(1, 256), jnp.int32)).astype(F32).reshape(1, 1024)
    place = jnp.stack([yhi, ylo, core, x]).astype(jnp.int32)

    halves = jnp.stack([matched >> 7, matched & 127], axis=2).reshape(128, 10).astype(BF)
    wide = jnp.concatenate([frames, jnp.pad(halves, ((0, 0), (0, PAD - 10)))], axis=1)
    wide = lax.dynamic_slice_in_dim(wide, core * 64, 64, 0)
    across = lax.ppermute(wide, ("ylo", "yhi"), [(0, 3), (3, 0), (1, 2), (2, 1)])
    wide = jnp.concatenate([wide, across], axis=0)
    after = lax.ppermute(wide, "x", [((i + 1) % 4, i) for i in range(4)])
    before = lax.ppermute(wide, "x", [((i - 1) % 4, i) for i in range(4)])
    opposite = fetch(jnp.where(core == 0, after, before), ("x",), 4)

    even = behind(even, after, before)
    odd = fetch(even, Z, 16)
    far_even = swap(even, "core")
    far_odd = swap(odd, "core")

    rows, *video = pl.pallas_call(
        project_kernel,
        in_specs=[smem] + [vmem] * 4 + [pl.BlockSpec(memory_space=pltpu.HBM)],
        out_specs=[vmem] * 5,
        out_shape=[
            jax.ShapeDtypeStruct((512, 1280), BF),
            jax.ShapeDtypeStruct((512, PAD), BF),
            jax.ShapeDtypeStruct((512, 1024), F32),
            jax.ShapeDtypeStruct((512, 1024), BF),
            jax.ShapeDtypeStruct((512, 128), F32),
        ],
        scratch_shapes=[pltpu.VMEM((1280, 1024), BF), pltpu.SemaphoreType.DMA((4,))],
        compiler_params=PARAMS,
        cost_estimate=pl.CostEstimate(flops=2 * 512 * 1280 * 1024, bytes_accessed=9 * 2**20, transcendentals=0),
    )(place, wide, after, opposite, before, pltpu.with_memory_space_constraint(projector, pltpu.HBM))
    parts = pl.pallas_call(
        pair_kernel,
        in_specs=[smem] + [vmem] * 10,
        out_specs=vmem,
        out_shape=jax.ShapeDtypeStruct((16, 256, 128), BF),
        compiler_params=PARAMS,
        cost_estimate=pl.CostEstimate(flops=5 * 512 * 1024 * 1024, bytes_accessed=8 * 2**20, transcendentals=2**20),
    )(
        jnp.concatenate([coldness, offset]),
        *video,
        ids,
        column_order(),
        even,
        far_even,
        odd,
        far_odd,
    )

    terms = lax.all_to_all(parts, PLANE, 0, 0, tiled=True)
    mine = pl.pallas_call(
        sum_kernel, in_specs=[vmem], out_specs=vmem, out_shape=jax.ShapeDtypeStruct((256, 128), BF), compiler_params=PARAMS
    )(terms)
    keep, give = pl.pallas_call(
        weight_kernel,
        in_specs=[smem] + [vmem] * 3,
        out_specs=[vmem, vmem],
        out_shape=[jax.ShapeDtypeStruct((16, 8, 320), F32), jax.ShapeDtypeStruct((16, 8, 320), BF)],
        compiler_params=PARAMS,
    )(place, mine, swap(mine, "ylo"), rows)
    mine = pl.pallas_call(
        add_kernel,
        in_specs=[vmem, vmem],
        out_specs=vmem,
        out_shape=jax.ShapeDtypeStruct((16, 8, 320), BF),
        compiler_params=PARAMS,
    )(keep, swap(give, "core"))
    sums = lax.all_to_all(mine, Z, 0, 0, tiled=True)
    return jnp.sum(sums.astype(F32), axis=0).T


def solution(mesh):
    fine = Mesh(mesh.devices.reshape(SIZES), AXES)
    return jax.shard_map(
        local,
        mesh=fine,
        in_specs=(P(DP, None), P(), P(AXES, None), P(DP, None), P(), P()),
        out_specs=P(CHIP, DP),
        check_vma=False,
    )
```

```python
import jax
import jax.numpy as jnp
import numpy as np
from jax import lax
from jax.experimental import pallas as pl
from jax.experimental.pallas import tpu as pltpu
from jax.sharding import Mesh, PartitionSpec as P

BF = jnp.bfloat16
F32 = jnp.float32
AXES = ("ylo", "core", "zp", "par", "x", "yhi")
SIZES = (2, 2, 8, 2, 4, 2)
DP = ("zp", "par", "x", "yhi")
Z = ("zp", "par")
PLANE = ("x", "yhi", "ylo")
CHIP = ("ylo", "core")
PAD = 128
PARAMS = pltpu.CompilerParams(vmem_limit_bytes=18 * 2**20)
SMALL = pltpu.CompilerParams(vmem_limit_bytes=12 * 2**20)


def column_order():
    was = np.arange(1024)
    goes = (was // 8 % 8) * 128 + (was // 64) * 8 + was % 8
    return jnp.asarray(goes[:, None] == was[None, :], BF)


def copies_kernel(a_ref, out_ref, sems):
    copies = [pltpu.make_async_copy(a_ref, out_ref.at[i], sems.at[i]) for i in range(out_ref.shape[0])]
    for copy in copies:
        copy.start()
    for copy in copies:
        copy.wait()


def project_kernel(*refs):
    *x_refs, w_ref, unit_ref, unit_b_ref, mag_ref = refs
    x = jnp.concatenate([ref[:, : w_ref.shape[0]] for ref in x_refs], axis=0)
    projected = jnp.dot(x, w_ref[...], preferred_element_type=F32)
    mag = jnp.sqrt(jnp.sum(projected * projected, axis=1, keepdims=True) + 1e-06)
    unit = projected / mag
    unit_ref[...] = unit
    unit_b_ref[...] = unit.astype(BF)
    mag_ref[...] = jnp.broadcast_to(mag, mag_ref.shape)


def project(w, *blocks):
    vmem = pl.BlockSpec(memory_space=pltpu.VMEM)
    n = sum(block.shape[0] for block in blocks)
    return pl.pallas_call(
        project_kernel,
        in_specs=[vmem] * (len(blocks) + 1),
        out_specs=[vmem] * 3,
        out_shape=[
            jax.ShapeDtypeStruct((n, 1024), F32),
            jax.ShapeDtypeStruct((n, 1024), BF),
            jax.ShapeDtypeStruct((n, 128), F32),
        ],
        compiler_params=SMALL,
        cost_estimate=pl.CostEstimate(flops=2 * n * 1280 * 1024, bytes_accessed=4 * 2**20, transcendentals=0),
    )(*blocks, w)


def row_blocks(place_ref):
    x, yhi = place_ref[3], place_ref[0]
    for i, k in enumerate((0, 1, 3, 2)):
        for j in range(2):
            half = yhi if j == 0 else 1 - yhi
            yield 128 * i + 64 * j, lax.rem(x + k, 4) * 128 + half * 64


def pair_kernel(scale_ref, place_ref, *refs):
    x_refs, video, ids_ref, order_ref, audio_refs, out_ref = refs[:4], refs[4:13], refs[13], refs[14], refs[15:19], refs[19]
    unit, unit_b, mag = (jnp.concatenate([ref[...] for ref in video[i::3]], axis=0) for i in range(3))
    cold = scale_ref[0]
    offset = scale_ref[1]
    halves = jnp.concatenate([ref[:, 1280:] for ref in x_refs], axis=0).astype(F32)
    targets = [halves[:, 2 * p : 2 * p + 1] * 128.0 + halves[:, 2 * p + 1 : 2 * p + 2] for p in range(5)]
    total = None
    at = 0
    for audio_ref in audio_refs:
        audio = audio_ref[...]
        n = audio.shape[0]
        ids = ids_ref[:1, at : at + n]
        at += n
        sims = lax.dot_general(unit_b, audio, (((1,), (1,)), ((), ())), preferred_element_type=F32)
        logits = cold * sims + offset
        hit = None
        for target in targets:
            same = target == ids
            hit = same if hit is None else hit | same
        weight = (jax.nn.sigmoid(logits) - jnp.where(hit, 1.0, 0.0)).astype(BF)
        term = jnp.dot(weight, audio, preferred_element_type=F32)
        total = term if total is None else total + term
    grad = cold * total
    inner = jnp.sum(unit * grad, axis=1, keepdims=True)
    gp = ((grad - unit * inner) / mag[:, :1]).astype(BF)
    gp = jnp.dot(gp, order_ref[...], preferred_element_type=F32).astype(BF)
    for at, to in row_blocks(place_ref):
        rows = pl.ds(pl.multiple_of(lax.rem(to, 256), 64), 64)
        for t in range(8):
            out_ref[2 * t + to // 256, rows, :] = gp[at : at + 64, 128 * t : 128 * (t + 1)]


def sum_kernel(g_ref, out_ref):
    total = g_ref[0].astype(F32)
    for s in range(1, g_ref.shape[0]):
        total = total + g_ref[s].astype(F32)
    out_ref[...] = total.astype(BF)


def weight_kernel(place_ref, mine_ref, other_ref, *refs):
    *x_refs, keep_ref, give_ref, gp_ref = refs
    ylo = place_ref[1]
    lanes = pl.ds(pl.multiple_of(ylo * 640, 128), 640)
    for at, to in row_blocks(place_ref):
        rows = pl.ds(pl.multiple_of(lax.rem(to, 256), 64), 64)
        gp_ref[at : at + 64] = jnp.where(to // 256 == ylo, mine_ref[rows, :], other_ref[rows, :])
    part = None
    for i, x_ref in enumerate(x_refs):
        term = lax.dot_general(
            gp_ref[128 * i : 128 * (i + 1)], x_ref[:, lanes], (((0,), (0,)), ((), ())), preferred_element_type=F32
        )
        part = term if part is None else part + term
    first, second = (part[:, 320 * c : 320 * (c + 1)].reshape(16, 8, 320) for c in range(2))
    core = place_ref[2]
    keep_ref[...] = jnp.where(core == 0, first, second)
    give_ref[...] = jnp.where(core == 0, second, first).astype(BF)


def add_kernel(a_ref, b_ref, out_ref):
    out_ref[...] = (a_ref[...] + b_ref[...].astype(F32)).astype(BF)


def fetch(a, axes, n):
    perm = [((i + 1) % n, i) for i in range(n)] + [(n + (i - 1) % n, n + i) for i in range(n)]
    return lax.ppermute(a, ("core", *axes), perm)


def behind(a, *others):
    anywhere = pl.BlockSpec(memory_space=pl.ANY)
    return pl.pallas_call(
        lambda *refs: None,
        in_specs=[anywhere] * (1 + len(others)),
        out_specs=anywhere,
        out_shape=jax.ShapeDtypeStruct(a.shape, a.dtype),
        input_output_aliases={0: 0},
        compiler_params=pltpu.CompilerParams(vmem_limit_bytes=2**16),
    )(a, *others)


def swap(a, axis):
    return lax.ppermute(a, axis, [(0, 1), (1, 0)])


def local(frames, projector, sounds, matched, coldness, offset):
    ylo, core, zp, par, x, yhi = (lax.axis_index(a) for a in AXES)
    smem = pl.BlockSpec(memory_space=pltpu.SMEM)
    vmem = pl.BlockSpec(memory_space=pltpu.VMEM)

    eight = pl.pallas_call(
        copies_kernel,
        in_specs=[pl.BlockSpec(memory_space=pltpu.HBM)],
        out_specs=pl.BlockSpec(memory_space=pltpu.HBM),
        out_shape=jax.ShapeDtypeStruct((8, 32, 1024), BF),
        scratch_shapes=[pltpu.SemaphoreType.DMA((8,))],
        compiler_params=pltpu.CompilerParams(vmem_limit_bytes=2**20),
    )(pltpu.with_memory_space_constraint(sounds, pltpu.HBM))
    even = lax.all_to_all(eight, "zp", 0, 0, tiled=True).reshape(256, 1024)
    pars = jnp.stack([par, par, 1 - par, 1 - par])
    cores = jnp.stack([core, 1 - core, core, 1 - core])
    firsts = ylo * 8192 + cores * 4096 + pars * 256 + (2 * x + yhi) * 32
    inside = np.arange(8)[:, None] * 512 + np.arange(32)[None, :]
    ids = (firsts[:, None] + jnp.asarray(inside.reshape(1, 256), jnp.int32)).astype(F32).reshape(1, 1024)
    place = jnp.stack([yhi, ylo, core, x]).astype(jnp.int32)

    halves = jnp.stack([matched >> 7, matched & 127], axis=2).reshape(128, 10).astype(BF)
    wide = jnp.concatenate([frames, jnp.pad(halves, ((0, 0), (0, PAD - 10)))], axis=1)
    wide = lax.dynamic_slice_in_dim(wide, core * 64, 64, 0)
    across = lax.ppermute(wide, ("ylo", "yhi"), [(0, 3), (3, 0), (1, 2), (2, 1)])
    wide = jnp.concatenate([wide, across], axis=0)
    after = lax.ppermute(wide, "x", [((i + 1) % 4, i) for i in range(4)])
    before = lax.ppermute(wide, "x", [((i - 1) % 4, i) for i in range(4)])
    opposite = fetch(jnp.where(core == 0, after, before), ("x",), 4)

    early = project(projector, wide)
    even = behind(even, after, before, early[2])
    odd = fetch(even, Z, 16)
    far_even = swap(even, "core")
    far_odd = swap(odd, "core")

    video = (wide, after, before, opposite)
    units = [*early, *project(projector, after, before), *project(projector, opposite)]
    parts = pl.pallas_call(
        pair_kernel,
        in_specs=[smem, smem] + [vmem] * 19,
        out_specs=vmem,
        out_shape=jax.ShapeDtypeStruct((16, 256, 128), BF),
        compiler_params=PARAMS,
        cost_estimate=pl.CostEstimate(flops=5 * 512 * 1024 * 1024, bytes_accessed=8 * 2**20, transcendentals=2**20),
    )(
        jnp.concatenate([coldness, offset]),
        place,
        *video,
        *units,
        ids,
        column_order(),
        even,
        far_even,
        odd,
        far_odd,
    )

    terms = lax.all_to_all(parts, PLANE, 0, 0, tiled=True)
    mine = pl.pallas_call(
        sum_kernel, in_specs=[vmem], out_specs=vmem, out_shape=jax.ShapeDtypeStruct((256, 128), BF), compiler_params=SMALL
    )(terms)
    keep, give = pl.pallas_call(
        weight_kernel,
        in_specs=[smem] + [vmem] * 6,
        out_specs=[vmem, vmem],
        out_shape=[jax.ShapeDtypeStruct((16, 8, 320), F32), jax.ShapeDtypeStruct((16, 8, 320), BF)],
        scratch_shapes=[pltpu.VMEM((512, 128), BF)],
        compiler_params=SMALL,
    )(place, mine, swap(mine, "ylo"), *video)
    mine = pl.pallas_call(
        add_kernel,
        in_specs=[vmem, vmem],
        out_specs=vmem,
        out_shape=jax.ShapeDtypeStruct((16, 8, 320), BF),
        compiler_params=SMALL,
    )(keep, swap(give, "core"))
    sums = lax.all_to_all(mine, Z, 0, 0, tiled=True)
    return jnp.sum(sums.astype(F32), axis=0).T


def solution(mesh):
    fine = Mesh(mesh.devices.reshape(SIZES), AXES)
    return jax.shard_map(
        local,
        mesh=fine,
        in_specs=(P(DP, None), P(), P(AXES, None), P(DP, None), P(), P()),
        out_specs=P(CHIP, DP),
        check_vma=False,
    )
```

```python
import jax
import jax.numpy as jnp
import numpy as np
from jax import lax
from jax.experimental import pallas as pl
from jax.experimental.pallas import tpu as pltpu
from jax.sharding import Mesh, PartitionSpec as P

BF = jnp.bfloat16
F32 = jnp.float32
AXES = ("ylo", "core", "zp", "par", "x", "yhi")
SIZES = (2, 2, 8, 2, 4, 2)
DP = ("zp", "par", "x", "yhi")
Z = ("zp", "par")
PLANE = ("x", "yhi", "ylo")
CHIP = ("ylo", "core")
PAD = 128
PARAMS = pltpu.CompilerParams(vmem_limit_bytes=18 * 2**20)
SMALL = pltpu.CompilerParams(vmem_limit_bytes=12 * 2**20)


def column_order():
    was = np.arange(1024)
    goes = (was // 8 % 8) * 128 + (was // 64) * 8 + was % 8
    return jnp.asarray(goes[:, None] == was[None, :], BF)


def project_kernel(*refs):
    *x_refs, w_ref, unit_ref, unit_b_ref, mag_ref = refs
    x = jnp.concatenate([ref[:, : w_ref.shape[0]] for ref in x_refs], axis=0)
    projected = jnp.dot(x, w_ref[...], preferred_element_type=F32)
    mag = jnp.sqrt(jnp.sum(projected * projected, axis=1, keepdims=True) + 1e-06)
    unit = projected / mag
    unit_ref[...] = unit
    unit_b_ref[...] = unit.astype(BF)
    mag_ref[...] = jnp.broadcast_to(mag, mag_ref.shape)


def project(w, *blocks):
    vmem = pl.BlockSpec(memory_space=pltpu.VMEM)
    n = sum(block.shape[0] for block in blocks)
    return pl.pallas_call(
        project_kernel,
        in_specs=[vmem] * (len(blocks) + 1),
        out_specs=[vmem] * 3,
        out_shape=[
            jax.ShapeDtypeStruct((n, 1024), F32),
            jax.ShapeDtypeStruct((n, 1024), BF),
            jax.ShapeDtypeStruct((n, 128), F32),
        ],
        compiler_params=SMALL,
        cost_estimate=pl.CostEstimate(flops=2 * n * 1280 * 1024, bytes_accessed=4 * 2**20, transcendentals=0),
    )(*blocks, w)


def row_blocks(place_ref):
    x, yhi = place_ref[3], place_ref[0]
    for i, k in enumerate((0, 1, 3, 2)):
        for j in range(2):
            half = yhi if j == 0 else 1 - yhi
            yield 128 * i + 64 * j, lax.rem(x + k, 4) * 128 + half * 64


def pair_kernel(scale_ref, place_ref, *refs):
    x_refs, video, ids_ref, order_ref, audio_refs, out_ref = refs[:4], refs[4:13], refs[13], refs[14], refs[15:19], refs[19]
    unit, unit_b, mag = (jnp.concatenate([ref[...] for ref in video[i::3]], axis=0) for i in range(3))
    cold = scale_ref[0]
    offset = scale_ref[1]
    halves = jnp.concatenate([ref[:, 1280:] for ref in x_refs], axis=0).astype(F32)
    targets = [halves[:, 2 * p : 2 * p + 1] * 128.0 + halves[:, 2 * p + 1 : 2 * p + 2] for p in range(5)]
    total = None
    at = 0
    for audio_ref in audio_refs:
        audio = audio_ref[...]
        n = audio.shape[0]
        ids = ids_ref[:1, at : at + n]
        at += n
        sims = lax.dot_general(unit_b, audio, (((1,), (1,)), ((), ())), preferred_element_type=F32)
        logits = cold * sims + offset
        hit = None
        for target in targets:
            same = target == ids
            hit = same if hit is None else hit | same
        weight = (jax.nn.sigmoid(logits) - jnp.where(hit, 1.0, 0.0)).astype(BF)
        term = jnp.dot(weight, audio, preferred_element_type=F32)
        total = term if total is None else total + term
    grad = cold * total
    inner = jnp.sum(unit * grad, axis=1, keepdims=True)
    gp = ((grad - unit * inner) / mag[:, :1]).astype(BF)
    gp = jnp.dot(gp, order_ref[...], preferred_element_type=F32).astype(BF)
    for at, to in row_blocks(place_ref):
        rows = pl.ds(pl.multiple_of(lax.rem(to, 256), 64), 64)
        for t in range(8):
            out_ref[2 * t + to // 256, rows, :] = gp[at : at + 64, 128 * t : 128 * (t + 1)]


def sum_kernel(g_ref, out_ref):
    total = g_ref[0].astype(F32)
    for s in range(1, g_ref.shape[0]):
        total = total + g_ref[s].astype(F32)
    out_ref[...] = total.astype(BF)


def weight_kernel(place_ref, mine_ref, other_ref, *refs):
    *x_refs, keep_ref, give_ref, gp_ref = refs
    ylo = place_ref[1]
    lanes = pl.ds(pl.multiple_of(ylo * 640, 128), 640)
    for at, to in row_blocks(place_ref):
        rows = pl.ds(pl.multiple_of(lax.rem(to, 256), 64), 64)
        gp_ref[at : at + 64] = jnp.where(to // 256 == ylo, mine_ref[rows, :], other_ref[rows, :])
    x = jnp.concatenate([ref[:, lanes] for ref in x_refs], axis=0)
    part = lax.dot_general(gp_ref[...], x, (((0,), (0,)), ((), ())), preferred_element_type=F32)
    first, second = (part[:, 320 * c : 320 * (c + 1)].reshape(16, 8, 320) for c in range(2))
    core = place_ref[2]
    keep_ref[...] = jnp.where(core == 0, first, second)
    give_ref[...] = jnp.where(core == 0, second, first).astype(BF)


def add_kernel(a_ref, b_ref, out_ref):
    out_ref[...] = (a_ref[...] + b_ref[...].astype(F32)).astype(BF)


def fetch(a, axes, n):
    perm = [((i + 1) % n, i) for i in range(n)] + [(n + (i - 1) % n, n + i) for i in range(n)]
    return lax.ppermute(a, ("core", *axes), perm)


def behind(a, *others):
    anywhere = pl.BlockSpec(memory_space=pl.ANY)
    return pl.pallas_call(
        lambda *refs: None,
        in_specs=[anywhere] * (1 + len(others)),
        out_specs=anywhere,
        out_shape=jax.ShapeDtypeStruct(a.shape, a.dtype),
        input_output_aliases={0: 0},
        compiler_params=pltpu.CompilerParams(vmem_limit_bytes=2**16),
    )(a, *others)


def swap(a, axis):
    return lax.ppermute(a, axis, [(0, 1), (1, 0)])


def local(frames, projector, sounds, matched, coldness, offset):
    ylo, core, zp, par, x, yhi = (lax.axis_index(a) for a in AXES)
    smem = pl.BlockSpec(memory_space=pltpu.SMEM)
    vmem = pl.BlockSpec(memory_space=pltpu.VMEM)

    even = lax.all_to_all(jnp.broadcast_to(sounds[None], (8, 32, 1024)), "zp", 0, 0, tiled=True).reshape(256, 1024)
    pars = jnp.stack([par, par, 1 - par, 1 - par])
    cores = jnp.stack([core, 1 - core, core, 1 - core])
    firsts = ylo * 8192 + cores * 4096 + pars * 256 + (2 * x + yhi) * 32
    inside = np.arange(8)[:, None] * 512 + np.arange(32)[None, :]
    ids = (firsts[:, None] + jnp.asarray(inside.reshape(1, 256), jnp.int32)).astype(F32).reshape(1, 1024)
    place = jnp.stack([yhi, ylo, core, x]).astype(jnp.int32)

    halves = jnp.stack([matched >> 7, matched & 127], axis=2).reshape(128, 10).astype(BF)
    wide = jnp.concatenate([frames, jnp.pad(halves, ((0, 0), (0, PAD - 10)))], axis=1)
    wide = lax.dynamic_slice_in_dim(wide, core * 64, 64, 0)
    across = lax.ppermute(wide, ("ylo", "yhi"), [(0, 3), (3, 0), (1, 2), (2, 1)])
    wide = jnp.concatenate([wide, across], axis=0)
    after = lax.ppermute(wide, "x", [((i + 1) % 4, i) for i in range(4)])
    before = lax.ppermute(wide, "x", [((i - 1) % 4, i) for i in range(4)])
    onward = jnp.where(core == 0, after, before)
    opposite = fetch(onward, ("x",), 4)

    early = project(projector, wide)
    scale = jnp.concatenate([coldness, offset])
    even = behind(even, after, before, early[2], ids, place, scale)
    odd = fetch(even, Z, 16)
    far_even = swap(even, "core")
    odd = behind(odd, opposite)
    far_odd = swap(odd, "core")

    video = (wide, after, before, opposite)
    units = [*early, *project(projector, after, before), *project(projector, opposite)]
    parts = pl.pallas_call(
        pair_kernel,
        in_specs=[smem, smem] + [vmem] * 19,
        out_specs=vmem,
        out_shape=jax.ShapeDtypeStruct((16, 256, 128), BF),
        compiler_params=PARAMS,
        cost_estimate=pl.CostEstimate(flops=5 * 512 * 1024 * 1024, bytes_accessed=8 * 2**20, transcendentals=2**20),
    )(
        scale,
        place,
        *video,
        *units,
        ids,
        column_order(),
        even,
        far_even,
        odd,
        far_odd,
    )

    terms = lax.all_to_all(parts, PLANE, 0, 0, tiled=True)
    mine = pl.pallas_call(
        sum_kernel, in_specs=[vmem], out_specs=vmem, out_shape=jax.ShapeDtypeStruct((256, 128), BF), compiler_params=SMALL
    )(terms)
    keep, give = pl.pallas_call(
        weight_kernel,
        in_specs=[smem] + [vmem] * 6,
        out_specs=[vmem, vmem],
        out_shape=[jax.ShapeDtypeStruct((16, 8, 320), F32), jax.ShapeDtypeStruct((16, 8, 320), BF)],
        scratch_shapes=[pltpu.VMEM((512, 128), BF)],
        compiler_params=SMALL,
    )(place, mine, swap(mine, "ylo"), *video)
    mine = pl.pallas_call(
        add_kernel,
        in_specs=[vmem, vmem],
        out_specs=vmem,
        out_shape=jax.ShapeDtypeStruct((16, 8, 320), BF),
        compiler_params=SMALL,
    )(keep, swap(give, "core"))
    sums = lax.all_to_all(mine, Z, 0, 0, tiled=True)
    return jnp.sum(sums.astype(F32), axis=0).T


def solution(mesh):
    fine = Mesh(mesh.devices.reshape(SIZES), AXES)
    return jax.shard_map(
        local,
        mesh=fine,
        in_specs=(P(DP, None), P(), P(AXES, None), P(DP, None), P(), P()),
        out_specs=P(CHIP, DP),
        check_vma=False,
    )
```

```python
import jax
import jax.numpy as jnp
import numpy as np
from jax import lax
from jax.experimental import pallas as pl
from jax.experimental.pallas import tpu as pltpu
from jax.sharding import Mesh, PartitionSpec as P

BF = jnp.bfloat16
F32 = jnp.float32
AXES = ("ylo", "core", "zp", "par", "x", "yhi")
SIZES = (2, 2, 8, 2, 4, 2)
DP = ("zp", "par", "x", "yhi")
Z = ("zp", "par")
PLANE = ("x", "yhi", "ylo")
CHIP = ("ylo", "core")
PAD = 128
PARAMS = pltpu.CompilerParams(vmem_limit_bytes=18 * 2**20)
SMALL = pltpu.CompilerParams(vmem_limit_bytes=12 * 2**20)


def column_order():
    was = np.arange(1024)
    goes = (was // 8 % 8) * 128 + (was // 64) * 8 + was % 8
    return jnp.asarray(goes[:, None] == was[None, :], BF)


def project_kernel(*refs):
    *x_refs, w_ref, unit_ref, unit_b_ref, mag_ref = refs
    x = jnp.concatenate([ref[:, : w_ref.shape[0]] for ref in x_refs], axis=0)
    projected = jnp.dot(x, w_ref[...], preferred_element_type=F32)
    mag = jnp.sqrt(jnp.sum(projected * projected, axis=1, keepdims=True) + 1e-06)
    unit = projected / mag
    unit_ref[...] = unit
    unit_b_ref[...] = unit.astype(BF)
    mag_ref[...] = jnp.broadcast_to(mag, mag_ref.shape)


def project(w, *blocks):
    vmem = pl.BlockSpec(memory_space=pltpu.VMEM)
    n = sum(block.shape[0] for block in blocks)
    return pl.pallas_call(
        project_kernel,
        in_specs=[vmem] * (len(blocks) + 1),
        out_specs=[vmem] * 3,
        out_shape=[
            jax.ShapeDtypeStruct((n, 1024), F32),
            jax.ShapeDtypeStruct((n, 1024), BF),
            jax.ShapeDtypeStruct((n, 128), F32),
        ],
        compiler_params=SMALL,
        cost_estimate=pl.CostEstimate(flops=2 * n * 1280 * 1024, bytes_accessed=4 * 2**20, transcendentals=0),
    )(*blocks, w)


def row_blocks(place_ref):
    x, yhi = place_ref[3], place_ref[0]
    for i, k in enumerate((0, 1, 3, 2)):
        for j in range(2):
            half = yhi if j == 0 else 1 - yhi
            yield 128 * i + 64 * j, lax.rem(x + k, 4) * 128 + half * 64


def pair_kernel(scale_ref, place_ref, *refs):
    x_refs, video, ids_ref, order_ref, audio_refs, out_ref = refs[:4], refs[4:13], refs[13], refs[14], refs[15:17], refs[17]
    unit, unit_b, mag = (jnp.concatenate([ref[...] for ref in video[i::3]], axis=0) for i in range(3))
    cold = scale_ref[0]
    offset = scale_ref[1]
    halves = jnp.concatenate([ref[:, 1280:] for ref in x_refs], axis=0).astype(F32)
    targets = [halves[:, 2 * p : 2 * p + 1] * 128.0 + halves[:, 2 * p + 1 : 2 * p + 2] for p in range(5)]
    total = None
    at = 0
    for audio_ref in audio_refs:
        audio = audio_ref[...]
        n = audio.shape[0]
        ids = ids_ref[:1, at : at + n]
        at += n
        sims = lax.dot_general(unit_b, audio, (((1,), (1,)), ((), ())), preferred_element_type=F32)
        logits = cold * sims + offset
        hit = None
        for target in targets:
            same = target == ids
            hit = same if hit is None else hit | same
        weight = (jax.nn.sigmoid(logits) - jnp.where(hit, 1.0, 0.0)).astype(BF)
        term = jnp.dot(weight, audio, preferred_element_type=F32)
        total = term if total is None else total + term
    grad = cold * total
    inner = jnp.sum(unit * grad, axis=1, keepdims=True)
    gp = ((grad - unit * inner) / mag[:, :1]).astype(BF)
    gp = jnp.dot(gp, order_ref[...], preferred_element_type=F32).astype(BF)
    for at, to in row_blocks(place_ref):
        rows = pl.ds(pl.multiple_of(lax.rem(to, 256), 64), 64)
        for t in range(8):
            out_ref[2 * t + to // 256, rows, :] = gp[at : at + 64, 128 * t : 128 * (t + 1)]


def sum_kernel(g_ref, out_ref):
    total = g_ref[0].astype(F32)
    for s in range(1, g_ref.shape[0]):
        total = total + g_ref[s].astype(F32)
    out_ref[...] = total.astype(BF)


def weight_kernel(place_ref, mine_ref, other_ref, *refs):
    *x_refs, keep_ref, give_ref, gp_ref = refs
    ylo = place_ref[1]
    lanes = pl.ds(pl.multiple_of(ylo * 640, 128), 640)
    for at, to in row_blocks(place_ref):
        rows = pl.ds(pl.multiple_of(lax.rem(to, 256), 64), 64)
        gp_ref[at : at + 64] = jnp.where(to // 256 == ylo, mine_ref[rows, :], other_ref[rows, :])
    x = jnp.concatenate([ref[:, lanes] for ref in x_refs], axis=0)
    part = lax.dot_general(gp_ref[...], x, (((0,), (0,)), ((), ())), preferred_element_type=F32)
    first, second = (part[:, 320 * c : 320 * (c + 1)].reshape(16, 8, 320) for c in range(2))
    core = place_ref[2]
    keep_ref[...] = jnp.where(core == 0, first, second)
    give_ref[...] = jnp.where(core == 0, second, first).astype(BF)


def add_kernel(a_ref, b_ref, out_ref):
    out_ref[...] = (a_ref[...] + b_ref[...].astype(F32)).astype(BF)


def fetch(a, axes, n):
    perm = [((i + 1) % n, i) for i in range(n)] + [(n + (i - 1) % n, n + i) for i in range(n)]
    return lax.ppermute(a, ("core", *axes), perm)


def behind(a, *others):
    anywhere = pl.BlockSpec(memory_space=pl.ANY)
    return pl.pallas_call(
        lambda *refs: None,
        in_specs=[anywhere] * (1 + len(others)),
        out_specs=anywhere,
        out_shape=jax.ShapeDtypeStruct(a.shape, a.dtype),
        input_output_aliases={0: 0},
        compiler_params=pltpu.CompilerParams(vmem_limit_bytes=2**16),
    )(a, *others)


def stack_kernel(a_ref, b_ref, *refs):
    out_ref = refs[-1]
    n = a_ref.shape[0]
    out_ref[:n] = a_ref[...]
    out_ref[n:] = b_ref[...]


def stack(a, b, *others):
    vmem = pl.BlockSpec(memory_space=pltpu.VMEM)
    return pl.pallas_call(
        stack_kernel,
        in_specs=[vmem, vmem] + [pl.BlockSpec(memory_space=pl.ANY)] * len(others),
        out_specs=vmem,
        out_shape=jax.ShapeDtypeStruct((a.shape[0] + b.shape[0], a.shape[1]), a.dtype),
        compiler_params=pltpu.CompilerParams(vmem_limit_bytes=4 * 2**20),
    )(a, b, *others)


def swap(a, axis):
    return lax.ppermute(a, axis, [(0, 1), (1, 0)])


def local(frames, projector, sounds, matched, coldness, offset):
    ylo, core, zp, par, x, yhi = (lax.axis_index(a) for a in AXES)
    smem = pl.BlockSpec(memory_space=pltpu.SMEM)
    vmem = pl.BlockSpec(memory_space=pltpu.VMEM)

    even = lax.all_to_all(jnp.broadcast_to(sounds[None], (8, 32, 1024)), "zp", 0, 0, tiled=True).reshape(256, 1024)
    pars = jnp.stack([par, 1 - par, par, 1 - par])
    cores = jnp.stack([core, core, 1 - core, 1 - core])
    firsts = ylo * 8192 + cores * 4096 + pars * 256 + (2 * x + yhi) * 32
    inside = np.arange(8)[:, None] * 512 + np.arange(32)[None, :]
    ids = (firsts[:, None] + jnp.asarray(inside.reshape(1, 256), jnp.int32)).astype(F32).reshape(1, 1024)
    place = jnp.stack([yhi, ylo, core, x]).astype(jnp.int32)

    halves = jnp.stack([matched >> 7, matched & 127], axis=2).reshape(128, 10).astype(BF)
    wide = jnp.concatenate([frames, jnp.pad(halves, ((0, 0), (0, PAD - 10)))], axis=1)
    wide = lax.dynamic_slice_in_dim(wide, core * 64, 64, 0)
    across = lax.ppermute(wide, ("ylo", "yhi"), [(0, 3), (3, 0), (1, 2), (2, 1)])
    wide = jnp.concatenate([wide, across], axis=0)
    after = lax.ppermute(wide, "x", [((i + 1) % 4, i) for i in range(4)])
    before = lax.ppermute(wide, "x", [((i - 1) % 4, i) for i in range(4)])
    onward = jnp.where(core == 0, after, before)
    opposite = fetch(onward, ("x",), 4)

    early = project(projector, wide)
    scale = jnp.concatenate([coldness, offset])
    even = behind(even, after, before, early[2], ids, place, scale)
    odd = fetch(even, Z, 16)
    late = project(projector, after, before)
    audio = stack(even, odd, opposite, late[2])
    far_audio = swap(audio, "core")

    video = (wide, after, before, opposite)
    units = [*early, *late, *project(projector, opposite)]
    parts = pl.pallas_call(
        pair_kernel,
        in_specs=[smem, smem] + [vmem] * 17,
        out_specs=vmem,
        out_shape=jax.ShapeDtypeStruct((16, 256, 128), BF),
        compiler_params=PARAMS,
        cost_estimate=pl.CostEstimate(flops=5 * 512 * 1024 * 1024, bytes_accessed=8 * 2**20, transcendentals=2**20),
    )(
        scale,
        place,
        *video,
        *units,
        ids,
        column_order(),
        audio,
        far_audio,
    )

    terms = lax.all_to_all(parts, PLANE, 0, 0, tiled=True)
    mine = pl.pallas_call(
        sum_kernel, in_specs=[vmem], out_specs=vmem, out_shape=jax.ShapeDtypeStruct((256, 128), BF), compiler_params=SMALL
    )(terms)
    keep, give = pl.pallas_call(
        weight_kernel,
        in_specs=[smem] + [vmem] * 6,
        out_specs=[vmem, vmem],
        out_shape=[jax.ShapeDtypeStruct((16, 8, 320), F32), jax.ShapeDtypeStruct((16, 8, 320), BF)],
        scratch_shapes=[pltpu.VMEM((512, 128), BF)],
        compiler_params=SMALL,
    )(place, mine, swap(mine, "ylo"), *video)
    mine = pl.pallas_call(
        add_kernel,
        in_specs=[vmem, vmem],
        out_specs=vmem,
        out_shape=jax.ShapeDtypeStruct((16, 8, 320), BF),
        compiler_params=SMALL,
    )(keep, swap(give, "core"))
    sums = lax.all_to_all(mine, Z, 0, 0, tiled=True)
    return jnp.sum(sums.astype(F32), axis=0).T


def solution(mesh):
    fine = Mesh(mesh.devices.reshape(SIZES), AXES)
    return jax.shard_map(
        local,
        mesh=fine,
        in_specs=(P(DP, None), P(), P(AXES, None), P(DP, None), P(), P()),
        out_specs=P(CHIP, DP),
        check_vma=False,
    )
```

```python
import jax
import jax.numpy as jnp
import numpy as np
from jax import lax
from jax.experimental import pallas as pl
from jax.experimental.pallas import tpu as pltpu
from jax.sharding import Mesh, PartitionSpec as P

BF = jnp.bfloat16
F32 = jnp.float32
AXES = ("ylo", "core", "zp", "par", "x", "yhi")
SIZES = (2, 2, 8, 2, 4, 2)
DP = ("zp", "par", "x", "yhi")
Z = ("zp", "par")
PLANE = ("x", "yhi", "ylo")
CHIP = ("ylo", "core")
PAD = 128
PARAMS = pltpu.CompilerParams(vmem_limit_bytes=18 * 2**20)
SMALL = pltpu.CompilerParams(vmem_limit_bytes=12 * 2**20)


def column_order():
    was = np.arange(1024)
    goes = (was // 8 % 8) * 128 + (was // 64) * 8 + was % 8
    return jnp.asarray(goes[:, None] == was[None, :], BF)


def project_kernel(*refs):
    *x_refs, w_ref, unit_ref, unit_b_ref, mag_ref = refs
    x = jnp.concatenate([ref[:, : w_ref.shape[0]] for ref in x_refs], axis=0)
    projected = jnp.dot(x, w_ref[...], preferred_element_type=F32)
    mag = jnp.sqrt(jnp.sum(projected * projected, axis=1, keepdims=True) + 1e-06)
    unit = projected / mag
    unit_ref[...] = unit
    unit_b_ref[...] = unit.astype(BF)
    mag_ref[...] = jnp.broadcast_to(mag, mag_ref.shape)


def project(w, *blocks):
    vmem = pl.BlockSpec(memory_space=pltpu.VMEM)
    n = sum(block.shape[0] for block in blocks)
    return pl.pallas_call(
        project_kernel,
        in_specs=[vmem] * (len(blocks) + 1),
        out_specs=[vmem] * 3,
        out_shape=[
            jax.ShapeDtypeStruct((n, 1024), F32),
            jax.ShapeDtypeStruct((n, 1024), BF),
            jax.ShapeDtypeStruct((n, 128), F32),
        ],
        compiler_params=SMALL,
        cost_estimate=pl.CostEstimate(flops=2 * n * 1280 * 1024, bytes_accessed=4 * 2**20, transcendentals=0),
    )(*blocks, w)


def row_blocks(place_ref):
    x, yhi = place_ref[3], place_ref[0]
    for i, k in enumerate((0, 1, 3, 2)):
        for j in range(2):
            half = yhi if j == 0 else 1 - yhi
            yield 128 * i + 64 * j, lax.rem(x + k, 4) * 128 + half * 64


def pairs(scale_ref, x_refs, unit_b_refs, ids, audio_ref):
    cold = scale_ref[0]
    offset = scale_ref[1]
    unit_b = jnp.concatenate([ref[...] for ref in unit_b_refs], axis=0)
    halves = jnp.concatenate([ref[:, 1280:] for ref in x_refs], axis=0).astype(F32)
    audio = audio_ref[...]
    sims = lax.dot_general(unit_b, audio, (((1,), (1,)), ((), ())), preferred_element_type=F32)
    logits = cold * sims + offset
    hit = None
    for p in range(5):
        target = halves[:, 2 * p : 2 * p + 1] * 128.0 + halves[:, 2 * p + 1 : 2 * p + 2]
        same = target == ids
        hit = same if hit is None else hit | same
    weight = (jax.nn.sigmoid(logits) - jnp.where(hit, 1.0, 0.0)).astype(BF)
    return jnp.dot(weight, audio, preferred_element_type=F32)


def own_kernel(scale_ref, *refs):
    refs[-1][...] = pairs(scale_ref, refs[:4], refs[4:7], refs[7][:, :512], refs[8])


def pair_kernel(scale_ref, place_ref, *refs):
    out_ref = refs[-1]
    units, unit_bs, mags = (refs[4 + i : 13 : 3] for i in range(3))
    ids_ref, audio_ref, own_ref, order_ref = refs[13:17]
    total = own_ref[...] + pairs(scale_ref, refs[:4], unit_bs, ids_ref[:, 512:], audio_ref)
    unit, mag = (jnp.concatenate([ref[...] for ref in part], axis=0) for part in (units, mags))
    grad = scale_ref[0] * total
    inner = jnp.sum(unit * grad, axis=1, keepdims=True)
    gp = ((grad - unit * inner) / mag[:, :1]).astype(BF)
    gp = jnp.dot(gp, order_ref[...], preferred_element_type=F32).astype(BF)
    for at, to in row_blocks(place_ref):
        rows = pl.ds(pl.multiple_of(lax.rem(to, 256), 64), 64)
        for t in range(8):
            out_ref[2 * t + to // 256, rows, :] = gp[at : at + 64, 128 * t : 128 * (t + 1)]


def sum_kernel(g_ref, out_ref):
    total = g_ref[0].astype(F32)
    for s in range(1, g_ref.shape[0]):
        total = total + g_ref[s].astype(F32)
    out_ref[...] = total.astype(BF)


def weight_kernel(place_ref, mine_ref, other_ref, *refs):
    *x_refs, keep_ref, give_ref, gp_ref = refs
    ylo = place_ref[1]
    lanes = pl.ds(pl.multiple_of(ylo * 640, 128), 640)
    for at, to in row_blocks(place_ref):
        rows = pl.ds(pl.multiple_of(lax.rem(to, 256), 64), 64)
        gp_ref[at : at + 64] = jnp.where(to // 256 == ylo, mine_ref[rows, :], other_ref[rows, :])
    x = jnp.concatenate([ref[:, lanes] for ref in x_refs], axis=0)
    part = lax.dot_general(gp_ref[...], x, (((0,), (0,)), ((), ())), preferred_element_type=F32)
    first, second = (part[:, 320 * c : 320 * (c + 1)].reshape(16, 8, 320) for c in range(2))
    core = place_ref[2]
    keep_ref[...] = jnp.where(core == 0, first, second)
    give_ref[...] = jnp.where(core == 0, second, first).astype(BF)


def add_kernel(a_ref, b_ref, out_ref):
    out_ref[...] = (a_ref[...] + b_ref[...].astype(F32)).astype(BF)


def fetch(a, axes, n):
    perm = [((i + 1) % n, i) for i in range(n)] + [(n + (i - 1) % n, n + i) for i in range(n)]
    return lax.ppermute(a, ("core", *axes), perm)


def behind(a, *others):
    anywhere = pl.BlockSpec(memory_space=pl.ANY)
    return pl.pallas_call(
        lambda *refs: None,
        in_specs=[anywhere] * (1 + len(others)),
        out_specs=anywhere,
        out_shape=jax.ShapeDtypeStruct(a.shape, a.dtype),
        input_output_aliases={0: 0},
        compiler_params=pltpu.CompilerParams(vmem_limit_bytes=2**16),
    )(a, *others)


def stack_kernel(a_ref, b_ref, *refs):
    out_ref = refs[-1]
    n = a_ref.shape[0]
    out_ref[:n] = a_ref[...]
    out_ref[n:] = b_ref[...]


def stack(a, b, *others):
    vmem = pl.BlockSpec(memory_space=pltpu.VMEM)
    return pl.pallas_call(
        stack_kernel,
        in_specs=[vmem, vmem] + [pl.BlockSpec(memory_space=pl.ANY)] * len(others),
        out_specs=vmem,
        out_shape=jax.ShapeDtypeStruct((a.shape[0] + b.shape[0], a.shape[1]), a.dtype),
        compiler_params=pltpu.CompilerParams(vmem_limit_bytes=4 * 2**20),
    )(a, b, *others)


def swap(a, axis):
    return lax.ppermute(a, axis, [(0, 1), (1, 0)])


def local(frames, projector, sounds, matched, coldness, offset):
    ylo, core, zp, par, x, yhi = (lax.axis_index(a) for a in AXES)
    smem = pl.BlockSpec(memory_space=pltpu.SMEM)
    vmem = pl.BlockSpec(memory_space=pltpu.VMEM)

    even = lax.all_to_all(jnp.broadcast_to(sounds[None], (8, 32, 1024)), "zp", 0, 0, tiled=True).reshape(256, 1024)
    pars = jnp.stack([par, 1 - par, par, 1 - par])
    cores = jnp.stack([core, core, 1 - core, 1 - core])
    firsts = ylo * 8192 + cores * 4096 + pars * 256 + (2 * x + yhi) * 32
    inside = np.arange(8)[:, None] * 512 + np.arange(32)[None, :]
    ids = (firsts[:, None] + jnp.asarray(inside.reshape(1, 256), jnp.int32)).astype(F32).reshape(1, 1024)
    place = jnp.stack([yhi, ylo, core, x]).astype(jnp.int32)

    halves = jnp.stack([matched >> 7, matched & 127], axis=2).reshape(128, 10).astype(BF)
    wide = jnp.concatenate([frames, jnp.pad(halves, ((0, 0), (0, PAD - 10)))], axis=1)
    wide = lax.dynamic_slice_in_dim(wide, core * 64, 64, 0)
    across = lax.ppermute(wide, ("ylo", "yhi"), [(0, 3), (3, 0), (1, 2), (2, 1)])
    wide = jnp.concatenate([wide, across], axis=0)
    after = lax.ppermute(wide, "x", [((i + 1) % 4, i) for i in range(4)])
    before = lax.ppermute(wide, "x", [((i - 1) % 4, i) for i in range(4)])
    onward = jnp.where(core == 0, after, before)
    opposite = fetch(onward, ("x",), 4)

    early = project(projector, wide)
    scale = jnp.concatenate([coldness, offset])
    even = behind(even, after, before, early[2], ids, place, scale)
    odd = fetch(even, Z, 16)
    late = project(projector, after, before)
    audio = stack(even, odd, opposite, late[2])
    far_audio = swap(audio, "core")

    video = (wide, after, before, opposite)
    units = [*early, *late, *project(projector, opposite)]
    own = pl.pallas_call(
        own_kernel,
        in_specs=[smem] + [vmem] * 9,
        out_specs=vmem,
        out_shape=jax.ShapeDtypeStruct((512, 1024), F32),
        compiler_params=PARAMS,
        cost_estimate=pl.CostEstimate(flops=2 * 512 * 1024 * 1024, bytes_accessed=4 * 2**20, transcendentals=2**19),
    )(scale, *video, *units[1::3], ids, audio)
    parts = pl.pallas_call(
        pair_kernel,
        in_specs=[smem, smem] + [vmem] * 17,
        out_specs=vmem,
        out_shape=jax.ShapeDtypeStruct((16, 256, 128), BF),
        compiler_params=PARAMS,
        cost_estimate=pl.CostEstimate(flops=3 * 512 * 1024 * 1024, bytes_accessed=8 * 2**20, transcendentals=2**19),
    )(scale, place, *video, *units, ids, far_audio, own, column_order())

    terms = lax.all_to_all(parts, PLANE, 0, 0, tiled=True)
    mine = pl.pallas_call(
        sum_kernel, in_specs=[vmem], out_specs=vmem, out_shape=jax.ShapeDtypeStruct((256, 128), BF), compiler_params=SMALL
    )(terms)
    keep, give = pl.pallas_call(
        weight_kernel,
        in_specs=[smem] + [vmem] * 6,
        out_specs=[vmem, vmem],
        out_shape=[jax.ShapeDtypeStruct((16, 8, 320), F32), jax.ShapeDtypeStruct((16, 8, 320), BF)],
        scratch_shapes=[pltpu.VMEM((512, 128), BF)],
        compiler_params=SMALL,
    )(place, mine, swap(mine, "ylo"), *video)
    mine = pl.pallas_call(
        add_kernel,
        in_specs=[vmem, vmem],
        out_specs=vmem,
        out_shape=jax.ShapeDtypeStruct((16, 8, 320), BF),
        compiler_params=SMALL,
    )(keep, swap(give, "core"))
    sums = lax.all_to_all(mine, Z, 0, 0, tiled=True)
    return jnp.sum(sums.astype(F32), axis=0).T


def solution(mesh):
    fine = Mesh(mesh.devices.reshape(SIZES), AXES)
    return jax.shard_map(
        local,
        mesh=fine,
        in_specs=(P(DP, None), P(), P(AXES, None), P(DP, None), P(), P()),
        out_specs=P(CHIP, DP),
        check_vma=False,
    )
```

```python
import jax
import jax.numpy as jnp
import numpy as np
from jax import lax
from jax.experimental import pallas as pl
from jax.experimental.pallas import tpu as pltpu
from jax.sharding import Mesh, PartitionSpec as P

BF = jnp.bfloat16
F32 = jnp.float32
AXES = ("ylo", "core", "zp", "par", "x", "yhi")
SIZES = (2, 2, 8, 2, 4, 2)
DP = ("zp", "par", "x", "yhi")
Z = ("zp", "par")
PLANE = ("x", "yhi", "ylo")
CHIP = ("ylo", "core")
PAD = 128
PARAMS = pltpu.CompilerParams(vmem_limit_bytes=18 * 2**20)


def column_order():
    was = np.arange(1024)
    goes = (was // 8 % 8) * 128 + (was // 64) * 8 + was % 8
    return jnp.asarray(goes[:, None] == was[None, :], BF)


def project_kernel(x_ref, w_ref, unit_ref, unit_b_ref, mag_ref):
    projected = jnp.dot(x_ref[:, : w_ref.shape[0]], w_ref[...], preferred_element_type=F32)
    mag = jnp.sqrt(jnp.sum(projected * projected, axis=1, keepdims=True) + 1e-06)
    unit = projected / mag
    unit_ref[...] = unit
    unit_b_ref[...] = unit.astype(BF)
    mag_ref[...] = jnp.broadcast_to(mag, mag_ref.shape)


def pair_kernel(scale_ref, x_ref, unit_ref, unit_b_ref, mag_ref, ids_ref, order_ref, *refs):
    *audio_refs, out_ref = refs
    cold = scale_ref[0]
    offset = scale_ref[1]
    unit_b = unit_b_ref[...]
    halves = x_ref[:, 1280:].astype(F32)
    targets = [halves[:, 2 * p : 2 * p + 1] * 128.0 + halves[:, 2 * p + 1 : 2 * p + 2] for p in range(5)]
    total = None
    at = 0
    for audio_ref in audio_refs:
        audio = audio_ref[...]
        n = audio.shape[0]
        ids = ids_ref[:1, at : at + n]
        at += n
        sims = lax.dot_general(unit_b, audio, (((1,), (1,)), ((), ())), preferred_element_type=F32)
        logits = cold * sims + offset
        hit = None
        for target in targets:
            same = target == ids
            hit = same if hit is None else hit | same
        weight = (jax.nn.sigmoid(logits) - jnp.where(hit, 1.0, 0.0)).astype(BF)
        term = jnp.dot(weight, audio, preferred_element_type=F32)
        total = term if total is None else total + term
    grad = cold * total
    unit = unit_ref[...]
    inner = jnp.sum(unit * grad, axis=1, keepdims=True)
    gp = ((grad - unit * inner) / mag_ref[:, :1]).astype(BF)
    gp = jnp.dot(gp, order_ref[...], preferred_element_type=F32).astype(BF)
    for h in range(2):
        for t in range(8):
            out_ref[2 * t + h] = gp[256 * h : 256 * (h + 1), 128 * t : 128 * (t + 1)]


def sum_kernel(g_ref, out_ref):
    total = g_ref[0].astype(F32)
    for s in range(1, g_ref.shape[0]):
        total = total + g_ref[s].astype(F32)
    out_ref[...] = total.astype(BF)


def weight_kernel(place_ref, mine_ref, other_ref, x_ref, keep_ref, give_ref):
    ylo = place_ref[1]
    lanes = pl.ds(pl.multiple_of(ylo * 640, 128), 640)
    part = None
    for gp_ref, half in ((mine_ref, ylo), (other_ref, 1 - ylo)):
        rows = x_ref[pl.ds(pl.multiple_of(half * 256, 256), 256), lanes]
        term = lax.dot_general(gp_ref[...], rows, (((0,), (0,)), ((), ())), preferred_element_type=F32)
        part = term if part is None else part + term
    first, second = (part[:, 320 * c : 320 * (c + 1)].reshape(16, 8, 320) for c in range(2))
    core = place_ref[2]
    keep_ref[...] = jnp.where(core == 0, first, second)
    give_ref[...] = jnp.where(core == 0, second, first).astype(BF)


def add_kernel(a_ref, b_ref, out_ref):
    out_ref[...] = (a_ref[...] + b_ref[...].astype(F32)).astype(BF)


def fetch(a):
    perm = [((i + 1) % 16, i) for i in range(16)] + [(16 + (i - 1) % 16, 16 + i) for i in range(16)]
    return lax.ppermute(a, ("core", *Z), perm)


def behind(a, *others):
    anywhere = pl.BlockSpec(memory_space=pl.ANY)
    return pl.pallas_call(
        lambda *refs: None,
        in_specs=[anywhere] * (1 + len(others)),
        out_specs=anywhere,
        out_shape=jax.ShapeDtypeStruct(a.shape, a.dtype),
        input_output_aliases={0: 0},
        compiler_params=pltpu.CompilerParams(vmem_limit_bytes=2**16),
    )(a, *others)


def swap(a, axis):
    return lax.ppermute(a, axis, [(0, 1), (1, 0)])


def local(frames, projector, sounds, matched, coldness, offset):
    ylo, core, zp, par, x, yhi = (lax.axis_index(a) for a in AXES)
    smem = pl.BlockSpec(memory_space=pltpu.SMEM)
    vmem = pl.BlockSpec(memory_space=pltpu.VMEM)

    pars = jnp.stack([par, par, 1 - par, 1 - par])
    cores = jnp.stack([core, 1 - core, core, 1 - core])
    firsts = ylo * 8192 + cores * 4096 + pars * 256 + (2 * x + yhi) * 32
    inside = np.arange(8)[:, None] * 512 + np.arange(32)[None, :]
    ids = (firsts[:, None] + jnp.asarray(inside.reshape(1, 256), jnp.int32)).astype(F32).reshape(1, 1024)
    place = jnp.stack([yhi, ylo, core, x]).astype(jnp.int32)
    scale = jnp.concatenate([coldness, offset])

    halves = jnp.stack([matched >> 7, matched & 127], axis=2).reshape(128, 10).astype(BF)
    wide = jnp.concatenate([frames, jnp.pad(halves, ((0, 0), (0, PAD - 10)))], axis=1)
    wide = lax.dynamic_slice_in_dim(wide, core * 64, 64, 0)
    rows = lax.all_to_all(jnp.broadcast_to(wide[None], (8, 64, 1280 + PAD)), ("x", "yhi"), 0, 0, tiled=True)
    rows = rows.reshape(512, 1280 + PAD)

    even = lax.all_gather(sounds, "zp", axis=0, tiled=True)
    even = behind(even, ids, place, scale)
    odd = fetch(even)
    far_even = swap(even, "core")
    units = pl.pallas_call(
        project_kernel,
        in_specs=[vmem] * 2,
        out_specs=[vmem] * 3,
        out_shape=[
            jax.ShapeDtypeStruct((512, 1024), F32),
            jax.ShapeDtypeStruct((512, 1024), BF),
            jax.ShapeDtypeStruct((512, 128), F32),
        ],
        compiler_params=PARAMS,
        cost_estimate=pl.CostEstimate(flops=2 * 512 * 1280 * 1024, bytes_accessed=9 * 2**20, transcendentals=0),
    )(rows, projector)
    odd = behind(odd, units[2])
    far_odd = swap(odd, "core")

    parts = pl.pallas_call(
        pair_kernel,
        in_specs=[smem] + [vmem] * 10,
        out_specs=vmem,
        out_shape=jax.ShapeDtypeStruct((16, 256, 128), BF),
        compiler_params=PARAMS,
        cost_estimate=pl.CostEstimate(flops=5 * 512 * 1024 * 1024, bytes_accessed=8 * 2**20, transcendentals=2**20),
    )(
        scale,
        rows,
        *units,
        ids,
        column_order(),
        even,
        far_even,
        odd,
        far_odd,
    )

    terms = lax.all_to_all(parts, PLANE, 0, 0, tiled=True)
    mine = pl.pallas_call(
        sum_kernel, in_specs=[vmem], out_specs=vmem, out_shape=jax.ShapeDtypeStruct((256, 128), BF), compiler_params=PARAMS
    )(terms)
    keep, give = pl.pallas_call(
        weight_kernel,
        in_specs=[smem] + [vmem] * 3,
        out_specs=[vmem, vmem],
        out_shape=[jax.ShapeDtypeStruct((16, 8, 320), F32), jax.ShapeDtypeStruct((16, 8, 320), BF)],
        compiler_params=PARAMS,
    )(place, mine, swap(mine, "ylo"), rows)
    mine = pl.pallas_call(
        add_kernel,
        in_specs=[vmem, vmem],
        out_specs=vmem,
        out_shape=jax.ShapeDtypeStruct((16, 8, 320), BF),
        compiler_params=PARAMS,
    )(keep, swap(give, "core"))
    sums = lax.all_to_all(mine, Z, 0, 0, tiled=True)
    return jnp.sum(sums.astype(F32), axis=0).T


def solution(mesh):
    fine = Mesh(mesh.devices.reshape(SIZES), AXES)
    return jax.shard_map(
        local,
        mesh=fine,
        in_specs=(P(DP, None), P(), P(AXES, None), P(DP, None), P(), P()),
        out_specs=P(CHIP, DP),
        check_vma=False,
    )
```

```python
import jax
import jax.numpy as jnp
import numpy as np
from jax import lax
from jax.experimental import pallas as pl
from jax.experimental.pallas import tpu as pltpu
from jax.sharding import Mesh, PartitionSpec as P

BF = jnp.bfloat16
F32 = jnp.float32
AXES = ("ylo", "core", "zp", "par", "x", "yhi")
SIZES = (2, 2, 8, 2, 4, 2)
DP = ("zp", "par", "x", "yhi")
Z = ("zp", "par")
PLANE = ("x", "yhi", "ylo")
CHIP = ("ylo", "core")
PAD = 128
PARAMS = pltpu.CompilerParams(vmem_limit_bytes=18 * 2**20)


def column_order():
    was = np.arange(1024)
    goes = (was // 8 % 8) * 128 + (was // 64) * 8 + was % 8
    return jnp.asarray(goes[:, None] == was[None, :], BF)


def project_kernel(x_ref, w_ref, unit_ref, unit_b_ref, mag_ref):
    projected = jnp.dot(x_ref[:, : w_ref.shape[0]], w_ref[...], preferred_element_type=F32)
    mag = jnp.sqrt(jnp.sum(projected * projected, axis=1, keepdims=True) + 1e-06)
    unit = projected / mag
    unit_ref[...] = unit
    unit_b_ref[...] = unit.astype(BF)
    mag_ref[...] = jnp.broadcast_to(mag, mag_ref.shape)


def pair_kernel(scale_ref, x_ref, unit_ref, unit_b_ref, mag_ref, ids_ref, order_ref, *refs):
    *audio_refs, out_ref = refs
    cold = scale_ref[0]
    offset = scale_ref[1]
    unit_b = unit_b_ref[...]
    halves = x_ref[:, 1280:].astype(F32)
    targets = [halves[:, 2 * p : 2 * p + 1] * 128.0 + halves[:, 2 * p + 1 : 2 * p + 2] for p in range(5)]
    total = None
    at = 0
    for audio_ref in audio_refs:
        audio = audio_ref[...]
        n = audio.shape[0]
        ids = ids_ref[:1, at : at + n]
        at += n
        sims = lax.dot_general(unit_b, audio, (((1,), (1,)), ((), ())), preferred_element_type=F32)
        logits = cold * sims + offset
        hit = None
        for target in targets:
            same = target == ids
            hit = same if hit is None else hit | same
        weight = (jax.nn.sigmoid(logits) - jnp.where(hit, 1.0, 0.0)).astype(BF)
        term = jnp.dot(weight, audio, preferred_element_type=F32)
        total = term if total is None else total + term
    grad = cold * total
    unit = unit_ref[...]
    inner = jnp.sum(unit * grad, axis=1, keepdims=True)
    gp = ((grad - unit * inner) / mag_ref[:, :1]).astype(BF)
    gp = jnp.dot(gp, order_ref[...], preferred_element_type=F32).astype(BF)
    for h in range(2):
        for t in range(8):
            out_ref[2 * t + h] = gp[256 * h : 256 * (h + 1), 128 * t : 128 * (t + 1)]


def sum_kernel(g_ref, out_ref):
    total = g_ref[0].astype(F32)
    for s in range(1, g_ref.shape[0]):
        total = total + g_ref[s].astype(F32)
    out_ref[...] = total.astype(BF)


def weight_kernel(place_ref, mine_ref, other_ref, x_ref, keep_ref, give_ref):
    ylo = place_ref[1]
    lanes = pl.ds(pl.multiple_of(ylo * 640, 128), 640)
    part = None
    for gp_ref, half in ((mine_ref, ylo), (other_ref, 1 - ylo)):
        rows = x_ref[pl.ds(pl.multiple_of(half * 256, 256), 256), lanes]
        term = lax.dot_general(gp_ref[...], rows, (((0,), (0,)), ((), ())), preferred_element_type=F32)
        part = term if part is None else part + term
    first, second = (part[:, 320 * c : 320 * (c + 1)].reshape(16, 8, 320) for c in range(2))
    core = place_ref[2]
    keep_ref[...] = jnp.where(core == 0, first, second)
    give_ref[...] = jnp.where(core == 0, second, first).astype(BF)


def add_kernel(a_ref, b_ref, out_ref):
    out_ref[...] = (a_ref[...] + b_ref[...].astype(F32)).astype(BF)


def fetch(a):
    perm = [((i + 1) % 16, i) for i in range(16)] + [(16 + (i - 1) % 16, 16 + i) for i in range(16)]
    return lax.ppermute(a, ("core", *Z), perm)


def behind(a, *others):
    anywhere = pl.BlockSpec(memory_space=pl.ANY)
    return pl.pallas_call(
        lambda *refs: None,
        in_specs=[anywhere] * (1 + len(others)),
        out_specs=anywhere,
        out_shape=jax.ShapeDtypeStruct(a.shape, a.dtype),
        input_output_aliases={0: 0},
        compiler_params=pltpu.CompilerParams(vmem_limit_bytes=2**16),
    )(a, *others)


def swap(a, axis):
    return lax.ppermute(a, axis, [(0, 1), (1, 0)])


def local(frames, projector, sounds, matched, coldness, offset):
    ylo, core, zp, par, x, yhi = (lax.axis_index(a) for a in AXES)
    smem = pl.BlockSpec(memory_space=pltpu.SMEM)
    vmem = pl.BlockSpec(memory_space=pltpu.VMEM)

    pars = jnp.stack([par, par, 1 - par, 1 - par])
    cores = jnp.stack([core, 1 - core, core, 1 - core])
    firsts = ylo * 8192 + cores * 4096 + pars * 256 + (2 * x + yhi) * 32
    inside = np.arange(8)[:, None] * 512 + np.arange(32)[None, :]
    ids = (firsts[:, None] + jnp.asarray(inside.reshape(1, 256), jnp.int32)).astype(F32).reshape(1, 1024)
    place = jnp.stack([yhi, ylo, core, x]).astype(jnp.int32)
    scale = jnp.concatenate([coldness, offset])

    even = lax.all_gather(sounds, "zp", axis=0, tiled=True)

    halves = jnp.stack([matched >> 7, matched & 127], axis=2).reshape(128, 10).astype(BF)
    wide = jnp.concatenate([frames, jnp.pad(halves, ((0, 0), (0, PAD - 10)))], axis=1)
    wide = lax.dynamic_slice_in_dim(wide, core * 64, 64, 0)
    wide = behind(wide, even)
    rows = lax.all_to_all(jnp.broadcast_to(wide[None], (8, 64, 1280 + PAD)), ("x", "yhi"), 0, 0, tiled=True)
    rows = rows.reshape(512, 1280 + PAD)

    odd = fetch(even)
    far_even = swap(even, "core")
    odd = behind(odd, ids, place, scale)
    units = pl.pallas_call(
        project_kernel,
        in_specs=[vmem] * 2,
        out_specs=[vmem] * 3,
        out_shape=[
            jax.ShapeDtypeStruct((512, 1024), F32),
            jax.ShapeDtypeStruct((512, 1024), BF),
            jax.ShapeDtypeStruct((512, 128), F32),
        ],
        compiler_params=PARAMS,
        cost_estimate=pl.CostEstimate(flops=2 * 512 * 1280 * 1024, bytes_accessed=9 * 2**20, transcendentals=0),
    )(rows, projector)
    far_odd = swap(odd, "core")

    parts = pl.pallas_call(
        pair_kernel,
        in_specs=[smem] + [vmem] * 10,
        out_specs=vmem,
        out_shape=jax.ShapeDtypeStruct((16, 256, 128), BF),
        compiler_params=PARAMS,
        cost_estimate=pl.CostEstimate(flops=5 * 512 * 1024 * 1024, bytes_accessed=8 * 2**20, transcendentals=2**20),
    )(
        scale,
        rows,
        *units,
        ids,
        column_order(),
        even,
        far_even,
        odd,
        far_odd,
    )

    terms = lax.all_to_all(parts, PLANE, 0, 0, tiled=True)
    mine = pl.pallas_call(
        sum_kernel, in_specs=[vmem], out_specs=vmem, out_shape=jax.ShapeDtypeStruct((256, 128), BF), compiler_params=PARAMS
    )(terms)
    keep, give = pl.pallas_call(
        weight_kernel,
        in_specs=[smem] + [vmem] * 3,
        out_specs=[vmem, vmem],
        out_shape=[jax.ShapeDtypeStruct((16, 8, 320), F32), jax.ShapeDtypeStruct((16, 8, 320), BF)],
        compiler_params=PARAMS,
    )(place, mine, swap(mine, "ylo"), rows)
    mine = pl.pallas_call(
        add_kernel,
        in_specs=[vmem, vmem],
        out_specs=vmem,
        out_shape=jax.ShapeDtypeStruct((16, 8, 320), BF),
        compiler_params=PARAMS,
    )(keep, swap(give, "core"))
    sums = lax.all_to_all(mine, Z, 0, 0, tiled=True)
    return jnp.sum(sums.astype(F32), axis=0).T


def solution(mesh):
    fine = Mesh(mesh.devices.reshape(SIZES), AXES)
    return jax.shard_map(
        local,
        mesh=fine,
        in_specs=(P(DP, None), P(), P(AXES, None), P(DP, None), P(), P()),
        out_specs=P(CHIP, DP),
        check_vma=False,
    )
```

```python
import jax
import jax.numpy as jnp
import numpy as np
from jax import lax
from jax.experimental import pallas as pl
from jax.experimental.pallas import tpu as pltpu
from jax.sharding import Mesh, PartitionSpec as P

BF = jnp.bfloat16
F32 = jnp.float32
AXES = ("ylo", "core", "zp", "par", "x", "yhi")
SIZES = (2, 2, 8, 2, 4, 2)
DP = ("zp", "par", "x", "yhi")
Z = ("zp", "par")
PLANE = ("x", "yhi", "ylo")
CHIP = ("ylo", "core")
PAD = 128
PARAMS = pltpu.CompilerParams(vmem_limit_bytes=18 * 2**20)


def column_order():
    was = np.arange(1024)
    goes = (was // 8 % 8) * 128 + (was // 64) * 8 + was % 8
    return jnp.asarray(goes[:, None] == was[None, :], BF)


def spread_kernel(core_ref, frames_ref, matched_ref, out_ref, held, sems):
    rows = pl.ds(pl.multiple_of(core_ref[0] * 64, 64), 64)
    load = pltpu.make_async_copy(frames_ref.at[rows], held.at[:, pl.ds(0, 1280)], sems.at[8])
    load.start()
    targets = matched_ref[rows, :]
    lane = lax.broadcasted_iota(jnp.int32, (64, PAD), 1)
    halves = jnp.zeros((64, PAD), jnp.int32)
    for p in range(5):
        target = targets[:, p : p + 1]
        halves = jnp.where(lane == 2 * p, target >> 7, halves)
        halves = jnp.where(lane == 2 * p + 1, target & 127, halves)
    held[:, 1280:] = halves.astype(F32).astype(BF)
    load.wait()
    copies = [pltpu.make_async_copy(held, out_ref.at[i], sems.at[i]) for i in range(8)]
    for copy in copies:
        copy.start()
    for copy in copies:
        copy.wait()


def project_kernel(x_ref, w_ref, unit_ref, unit_b_ref, mag_ref):
    projected = jnp.dot(x_ref[:, : w_ref.shape[0]], w_ref[...], preferred_element_type=F32)
    mag = jnp.sqrt(jnp.sum(projected * projected, axis=1, keepdims=True) + 1e-06)
    unit = projected / mag
    unit_ref[...] = unit
    unit_b_ref[...] = unit.astype(BF)
    mag_ref[...] = jnp.broadcast_to(mag, mag_ref.shape)


def pair_kernel(scale_ref, x_ref, unit_ref, unit_b_ref, mag_ref, ids_ref, order_ref, *refs):
    *audio_refs, out_ref = refs
    cold = scale_ref[0]
    offset = scale_ref[1]
    unit_b = unit_b_ref[...]
    halves = x_ref[:, 1280:].astype(F32)
    targets = [halves[:, 2 * p : 2 * p + 1] * 128.0 + halves[:, 2 * p + 1 : 2 * p + 2] for p in range(5)]
    total = None
    at = 0
    for audio_ref in audio_refs:
        audio = audio_ref[...]
        n = audio.shape[0]
        ids = ids_ref[:1, at : at + n]
        at += n
        sims = lax.dot_general(unit_b, audio, (((1,), (1,)), ((), ())), preferred_element_type=F32)
        logits = cold * sims + offset
        hit = None
        for target in targets:
            same = target == ids
            hit = same if hit is None else hit | same
        weight = (jax.nn.sigmoid(logits) - jnp.where(hit, 1.0, 0.0)).astype(BF)
        term = jnp.dot(weight, audio, preferred_element_type=F32)
        total = term if total is None else total + term
    grad = cold * total
    unit = unit_ref[...]
    inner = jnp.sum(unit * grad, axis=1, keepdims=True)
    gp = ((grad - unit * inner) / mag_ref[:, :1]).astype(BF)
    gp = jnp.dot(gp, order_ref[...], preferred_element_type=F32).astype(BF)
    for h in range(2):
        for t in range(8):
            out_ref[2 * t + h] = gp[256 * h : 256 * (h + 1), 128 * t : 128 * (t + 1)]


def sum_kernel(g_ref, out_ref):
    total = g_ref[0].astype(F32)
    for s in range(1, g_ref.shape[0]):
        total = total + g_ref[s].astype(F32)
    out_ref[...] = total.astype(BF)


def weight_kernel(place_ref, mine_ref, other_ref, x_ref, keep_ref, give_ref):
    ylo = place_ref[1]
    lanes = pl.ds(pl.multiple_of(ylo * 640, 128), 640)
    part = None
    for gp_ref, half in ((mine_ref, ylo), (other_ref, 1 - ylo)):
        rows = x_ref[pl.ds(pl.multiple_of(half * 256, 256), 256), lanes]
        term = lax.dot_general(gp_ref[...], rows, (((0,), (0,)), ((), ())), preferred_element_type=F32)
        part = term if part is None else part + term
    first, second = (part[:, 320 * c : 320 * (c + 1)].reshape(16, 8, 320) for c in range(2))
    core = place_ref[2]
    keep_ref[...] = jnp.where(core == 0, first, second)
    give_ref[...] = jnp.where(core == 0, second, first).astype(BF)


def add_kernel(a_ref, b_ref, out_ref):
    out_ref[...] = (a_ref[...] + b_ref[...].astype(F32)).astype(BF)


def fetch(a):
    perm = [((i + 1) % 16, i) for i in range(16)] + [(16 + (i - 1) % 16, 16 + i) for i in range(16)]
    return lax.ppermute(a, ("core", *Z), perm)


def behind(a, *others):
    anywhere = pl.BlockSpec(memory_space=pl.ANY)
    return pl.pallas_call(
        lambda *refs: None,
        in_specs=[anywhere] * (1 + len(others)),
        out_specs=anywhere,
        out_shape=jax.ShapeDtypeStruct(a.shape, a.dtype),
        input_output_aliases={0: 0},
        compiler_params=pltpu.CompilerParams(vmem_limit_bytes=2**16),
    )(a, *others)


def swap(a, axis):
    return lax.ppermute(a, axis, [(0, 1), (1, 0)])


def local(frames, projector, sounds, matched, coldness, offset):
    ylo, core, zp, par, x, yhi = (lax.axis_index(a) for a in AXES)
    smem = pl.BlockSpec(memory_space=pltpu.SMEM)
    vmem = pl.BlockSpec(memory_space=pltpu.VMEM)

    pars = jnp.stack([par, par, 1 - par, 1 - par])
    cores = jnp.stack([core, 1 - core, core, 1 - core])
    firsts = ylo * 8192 + cores * 4096 + pars * 256 + (2 * x + yhi) * 32
    inside = np.arange(8)[:, None] * 512 + np.arange(32)[None, :]
    ids = (firsts[:, None] + jnp.asarray(inside.reshape(1, 256), jnp.int32)).astype(F32).reshape(1, 1024)
    place = jnp.stack([yhi, ylo, core, x]).astype(jnp.int32)
    scale = jnp.concatenate([coldness, offset])

    wide = pl.pallas_call(
        spread_kernel,
        in_specs=[smem, pl.BlockSpec(memory_space=pltpu.HBM), vmem],
        out_specs=pl.BlockSpec(memory_space=pltpu.HBM),
        out_shape=jax.ShapeDtypeStruct((8, 64, 1280 + PAD), BF),
        scratch_shapes=[pltpu.VMEM((64, 1280 + PAD), BF), pltpu.SemaphoreType.DMA((9,))],
        compiler_params=pltpu.CompilerParams(vmem_limit_bytes=4 * 2**20),
    )(core.reshape(1).astype(jnp.int32), pltpu.with_memory_space_constraint(frames, pltpu.HBM), matched)
    rows = lax.all_to_all(wide, ("x", "yhi"), 0, 0, tiled=True)
    rows = rows.reshape(512, 1280 + PAD)

    even = lax.all_gather(sounds, "zp", axis=0, tiled=True)
    odd = fetch(even)
    far_even = swap(even, "core")
    units = pl.pallas_call(
        project_kernel,
        in_specs=[vmem] * 2,
        out_specs=[vmem] * 3,
        out_shape=[
            jax.ShapeDtypeStruct((512, 1024), F32),
            jax.ShapeDtypeStruct((512, 1024), BF),
            jax.ShapeDtypeStruct((512, 128), F32),
        ],
        compiler_params=PARAMS,
        cost_estimate=pl.CostEstimate(flops=2 * 512 * 1280 * 1024, bytes_accessed=9 * 2**20, transcendentals=0),
    )(rows, projector)
    odd = behind(odd, units[2], ids, place, scale)
    far_odd = swap(odd, "core")

    parts = pl.pallas_call(
        pair_kernel,
        in_specs=[smem] + [vmem] * 10,
        out_specs=vmem,
        out_shape=jax.ShapeDtypeStruct((16, 256, 128), BF),
        compiler_params=PARAMS,
        cost_estimate=pl.CostEstimate(flops=5 * 512 * 1024 * 1024, bytes_accessed=8 * 2**20, transcendentals=2**20),
    )(
        scale,
        rows,
        *units,
        ids,
        column_order(),
        even,
        far_even,
        odd,
        far_odd,
    )

    terms = lax.all_to_all(parts, PLANE, 0, 0, tiled=True)
    mine = pl.pallas_call(
        sum_kernel, in_specs=[vmem], out_specs=vmem, out_shape=jax.ShapeDtypeStruct((256, 128), BF), compiler_params=PARAMS
    )(terms)
    keep, give = pl.pallas_call(
        weight_kernel,
        in_specs=[smem] + [vmem] * 3,
        out_specs=[vmem, vmem],
        out_shape=[jax.ShapeDtypeStruct((16, 8, 320), F32), jax.ShapeDtypeStruct((16, 8, 320), BF)],
        compiler_params=PARAMS,
    )(place, mine, swap(mine, "ylo"), rows)
    mine = pl.pallas_call(
        add_kernel,
        in_specs=[vmem, vmem],
        out_specs=vmem,
        out_shape=jax.ShapeDtypeStruct((16, 8, 320), BF),
        compiler_params=PARAMS,
    )(keep, swap(give, "core"))
    sums = lax.all_to_all(mine, Z, 0, 0, tiled=True)
    return jnp.sum(sums.astype(F32), axis=0).T


def solution(mesh):
    fine = Mesh(mesh.devices.reshape(SIZES), AXES)
    return jax.shard_map(
        local,
        mesh=fine,
        in_specs=(P(DP, None), P(), P(AXES, None), P(DP, None), P(), P()),
        out_specs=P(CHIP, DP),
        check_vma=False,
    )
```

```python
import jax
import jax.numpy as jnp
import numpy as np
from jax import lax
from jax.experimental import pallas as pl
from jax.experimental.pallas import tpu as pltpu
from jax.sharding import Mesh, PartitionSpec as P

BF = jnp.bfloat16
F32 = jnp.float32
AXES = ("ylo", "core", "zp", "par", "x", "yhi")
SIZES = (2, 2, 8, 2, 4, 2)
DP = ("zp", "par", "x", "yhi")
Z = ("zp", "par")
PLANE = ("x", "yhi", "ylo")
CHIP = ("ylo", "core")
PAD = 128
PARAMS = pltpu.CompilerParams(vmem_limit_bytes=18 * 2**20)


def column_order():
    was = np.arange(1024)
    goes = (was // 8 % 8) * 128 + (was // 64) * 8 + was % 8
    return jnp.asarray(goes[:, None] == was[None, :], BF)


def spread_kernel(core_ref, frames_ref, matched_ref, out_ref, held, sems):
    rows = pl.ds(pl.multiple_of(core_ref[0] * 64, 64), 64)
    load = pltpu.make_async_copy(frames_ref.at[rows], held.at[:, pl.ds(0, 1280)], sems.at[8])
    load.start()
    targets = matched_ref[rows, :]
    lane = lax.broadcasted_iota(jnp.int32, (64, PAD), 1)
    halves = jnp.zeros((64, PAD), jnp.int32)
    for p in range(5):
        target = targets[:, p : p + 1]
        halves = jnp.where(lane == 2 * p, target >> 7, halves)
        halves = jnp.where(lane == 2 * p + 1, target & 127, halves)
    held[:, 1280:] = halves.astype(F32).astype(BF)
    load.wait()
    copies = [pltpu.make_async_copy(held, out_ref.at[i], sems.at[i]) for i in range(8)]
    for copy in copies:
        copy.start()
    for copy in copies:
        copy.wait()


def project_kernel(x_ref, w_ref, unit_ref, unit_b_ref, mag_ref):
    projected = jnp.dot(x_ref[:, : w_ref.shape[0]], w_ref[...], preferred_element_type=F32)
    mag = jnp.sqrt(jnp.sum(projected * projected, axis=1, keepdims=True) + 1e-06)
    unit = projected / mag
    unit_ref[...] = unit
    unit_b_ref[...] = unit.astype(BF)
    mag_ref[...] = jnp.broadcast_to(mag, mag_ref.shape)


def pair_kernel(cold_ref, offset_ref, place_ref, x_ref, unit_ref, unit_b_ref, mag_ref, order_ref, *refs):
    *audio_refs, out_ref = refs
    cold = cold_ref[0]
    offset = offset_ref[0]
    yhi, ylo, core, x, par = (place_ref[i] for i in range(5))
    unit_b = unit_b_ref[...]
    halves = x_ref[:, 1280:].astype(F32)
    targets = [halves[:, 2 * p : 2 * p + 1] * 128.0 + halves[:, 2 * p + 1 : 2 * p + 2] for p in range(5)]
    total = None
    lane = lax.broadcasted_iota(jnp.int32, (1, 256), 1)
    inside = (lane >> 5) * 512 + (lane & 31)
    for side, audio_ref in enumerate(audio_refs):
        audio = audio_ref[...]
        on = core if side % 2 == 0 else 1 - core
        odd = par if side < 2 else 1 - par
        ids = (inside + (ylo * 8192 + on * 4096 + odd * 256 + (2 * x + yhi) * 32)).astype(F32)
        sims = lax.dot_general(unit_b, audio, (((1,), (1,)), ((), ())), preferred_element_type=F32)
        logits = cold * sims + offset
        hit = None
        for target in targets:
            same = target == ids
            hit = same if hit is None else hit | same
        weight = (jax.nn.sigmoid(logits) - jnp.where(hit, 1.0, 0.0)).astype(BF)
        term = jnp.dot(weight, audio, preferred_element_type=F32)
        total = term if total is None else total + term
    grad = cold * total
    unit = unit_ref[...]
    inner = jnp.sum(unit * grad, axis=1, keepdims=True)
    gp = ((grad - unit * inner) / mag_ref[:, :1]).astype(BF)
    gp = jnp.dot(gp, order_ref[...], preferred_element_type=F32).astype(BF)
    for h in range(2):
        for t in range(8):
            out_ref[2 * t + h] = gp[256 * h : 256 * (h + 1), 128 * t : 128 * (t + 1)]


def sum_kernel(g_ref, out_ref):
    total = g_ref[0].astype(F32)
    for s in range(1, g_ref.shape[0]):
        total = total + g_ref[s].astype(F32)
    out_ref[...] = total.astype(BF)


def weight_kernel(place_ref, mine_ref, other_ref, x_ref, keep_ref, give_ref):
    ylo = place_ref[1]
    lanes = pl.ds(pl.multiple_of(ylo * 640, 128), 640)
    part = None
    for gp_ref, half in ((mine_ref, ylo), (other_ref, 1 - ylo)):
        rows = x_ref[pl.ds(pl.multiple_of(half * 256, 256), 256), lanes]
        term = lax.dot_general(gp_ref[...], rows, (((0,), (0,)), ((), ())), preferred_element_type=F32)
        part = term if part is None else part + term
    first, second = (part[:, 320 * c : 320 * (c + 1)].reshape(16, 8, 320) for c in range(2))
    core = place_ref[2]
    keep_ref[...] = jnp.where(core == 0, first, second)
    give_ref[...] = jnp.where(core == 0, second, first).astype(BF)


def add_kernel(a_ref, b_ref, out_ref):
    out_ref[...] = (a_ref[...] + b_ref[...].astype(F32)).astype(BF)


def fetch(a):
    perm = [((i + 1) % 16, i) for i in range(16)] + [(16 + (i - 1) % 16, 16 + i) for i in range(16)]
    return lax.ppermute(a, ("core", *Z), perm)


def behind(a, *others):
    anywhere = pl.BlockSpec(memory_space=pl.ANY)
    return pl.pallas_call(
        lambda *refs: None,
        in_specs=[anywhere] * (1 + len(others)),
        out_specs=anywhere,
        out_shape=jax.ShapeDtypeStruct(a.shape, a.dtype),
        input_output_aliases={0: 0},
        compiler_params=pltpu.CompilerParams(vmem_limit_bytes=2**16),
    )(a, *others)


def swap(a, axis):
    return lax.ppermute(a, axis, [(0, 1), (1, 0)])


def local(frames, projector, sounds, matched, coldness, offset):
    ylo, core, zp, par, x, yhi = (lax.axis_index(a) for a in AXES)
    smem = pl.BlockSpec(memory_space=pltpu.SMEM)
    vmem = pl.BlockSpec(memory_space=pltpu.VMEM)

    place = jnp.stack([yhi, ylo, core, x, par]).astype(jnp.int32)

    wide = pl.pallas_call(
        spread_kernel,
        in_specs=[smem, pl.BlockSpec(memory_space=pltpu.HBM), vmem],
        out_specs=pl.BlockSpec(memory_space=pltpu.HBM),
        out_shape=jax.ShapeDtypeStruct((8, 64, 1280 + PAD), BF),
        scratch_shapes=[pltpu.VMEM((64, 1280 + PAD), BF), pltpu.SemaphoreType.DMA((9,))],
        compiler_params=pltpu.CompilerParams(vmem_limit_bytes=4 * 2**20),
    )(core.reshape(1).astype(jnp.int32), pltpu.with_memory_space_constraint(frames, pltpu.HBM), matched)
    rows = lax.all_to_all(wide, ("x", "yhi"), 0, 0, tiled=True)
    rows = rows.reshape(512, 1280 + PAD)

    even = lax.all_gather(sounds, "zp", axis=0, tiled=True)
    odd = fetch(even)
    far_even = swap(even, "core")
    units = pl.pallas_call(
        project_kernel,
        in_specs=[vmem] * 2,
        out_specs=[vmem] * 3,
        out_shape=[
            jax.ShapeDtypeStruct((512, 1024), F32),
            jax.ShapeDtypeStruct((512, 1024), BF),
            jax.ShapeDtypeStruct((512, 128), F32),
        ],
        compiler_params=PARAMS,
        cost_estimate=pl.CostEstimate(flops=2 * 512 * 1280 * 1024, bytes_accessed=9 * 2**20, transcendentals=0),
    )(rows, projector)
    odd = behind(odd, units[2], place)
    far_odd = swap(odd, "core")

    parts = pl.pallas_call(
        pair_kernel,
        in_specs=[smem] * 3 + [vmem] * 9,
        out_specs=vmem,
        out_shape=jax.ShapeDtypeStruct((16, 256, 128), BF),
        compiler_params=PARAMS,
        cost_estimate=pl.CostEstimate(flops=5 * 512 * 1024 * 1024, bytes_accessed=8 * 2**20, transcendentals=2**20),
    )(
        coldness,
        offset,
        place,
        rows,
        *units,
        column_order(),
        even,
        far_even,
        odd,
        far_odd,
    )

    terms = lax.all_to_all(parts, PLANE, 0, 0, tiled=True)
    mine = pl.pallas_call(
        sum_kernel, in_specs=[vmem], out_specs=vmem, out_shape=jax.ShapeDtypeStruct((256, 128), BF), compiler_params=PARAMS
    )(terms)
    keep, give = pl.pallas_call(
        weight_kernel,
        in_specs=[smem] + [vmem] * 3,
        out_specs=[vmem, vmem],
        out_shape=[jax.ShapeDtypeStruct((16, 8, 320), F32), jax.ShapeDtypeStruct((16, 8, 320), BF)],
        compiler_params=PARAMS,
    )(place, mine, swap(mine, "ylo"), rows)
    mine = pl.pallas_call(
        add_kernel,
        in_specs=[vmem, vmem],
        out_specs=vmem,
        out_shape=jax.ShapeDtypeStruct((16, 8, 320), BF),
        compiler_params=PARAMS,
    )(keep, swap(give, "core"))
    sums = lax.all_to_all(mine, Z, 0, 0, tiled=True)
    return jnp.sum(sums.astype(F32), axis=0).T


def solution(mesh):
    fine = Mesh(mesh.devices.reshape(SIZES), AXES)
    return jax.shard_map(
        local,
        mesh=fine,
        in_specs=(P(DP, None), P(), P(AXES, None), P(DP, None), P(), P()),
        out_specs=P(CHIP, DP),
        check_vma=False,
    )
```

```python
import jax
import jax.numpy as jnp
import numpy as np
from jax import lax
from jax.experimental import pallas as pl
from jax.experimental.pallas import tpu as pltpu
from jax.sharding import Mesh, PartitionSpec as P

BF = jnp.bfloat16
F32 = jnp.float32
AXES = ("ylo", "core", "zp", "par", "x", "yhi")
SIZES = (2, 2, 8, 2, 4, 2)
DP = ("zp", "par", "x", "yhi")
Z = ("zp", "par")
PLANE = ("x", "yhi", "ylo")
CHIP = ("ylo", "core")
PAD = 128
PARAMS = pltpu.CompilerParams(vmem_limit_bytes=18 * 2**20)


def column_order():
    was = np.arange(1024)
    goes = (was // 8 % 8) * 128 + (was // 64) * 8 + was % 8
    return jnp.asarray(goes[:, None] == was[None, :], BF)


def spread_kernel(core_ref, frames_ref, matched_ref, out_ref, held, listed, sems):
    rows = pl.ds(pl.multiple_of(core_ref[0] * 64, 64), 64)
    load = pltpu.make_async_copy(frames_ref.at[rows], held.at[:, pl.ds(0, 1280)], sems.at[8])
    load.start()
    fetch_targets = pltpu.make_async_copy(matched_ref, listed, sems.at[9])
    fetch_targets.start()
    fetch_targets.wait()
    targets = listed[...]
    lane = lax.broadcasted_iota(jnp.int32, (5, PAD), 1)
    twice = lax.broadcasted_iota(jnp.int32, (5, PAD), 0) * 2
    halves = None
    for i, part in enumerate((targets >> 7, targets & 127)):
        column = jnp.where(lane == twice + i, 1.0, 0.0).astype(BF)
        term = lax.dot_general(
            part.astype(F32).astype(BF), column, (((0,), (0,)), ((), ())), preferred_element_type=F32
        )
        halves = term if halves is None else halves + term
    held[:, 1280:] = jnp.where(core_ref[0] == 0, halves[:64], halves[64:]).astype(BF)
    load.wait()
    copies = [pltpu.make_async_copy(held, out_ref.at[i], sems.at[i]) for i in range(8)]
    for copy in copies:
        copy.start()
    for copy in copies:
        copy.wait()


def project_kernel(x_ref, w_ref, unit_ref, unit_b_ref, mag_ref):
    projected = jnp.dot(x_ref[:, : w_ref.shape[0]], w_ref[...], preferred_element_type=F32)
    mag = jnp.sqrt(jnp.sum(projected * projected, axis=1, keepdims=True) + 1e-06)
    unit = projected / mag
    unit_ref[...] = unit
    unit_b_ref[...] = unit.astype(BF)
    mag_ref[...] = jnp.broadcast_to(mag, mag_ref.shape)


def pair_kernel(cold_ref, offset_ref, place_ref, x_ref, unit_ref, unit_b_ref, mag_ref, order_ref, *refs):
    *audio_refs, out_ref = refs
    cold = cold_ref[0]
    offset = offset_ref[0]
    yhi, ylo, core, x, par = (place_ref[i] for i in range(5))
    unit_b = unit_b_ref[...]
    halves = x_ref[:, 1280:].astype(F32)
    targets = [halves[:, 2 * p : 2 * p + 1] * 128.0 + halves[:, 2 * p + 1 : 2 * p + 2] for p in range(5)]
    total = None
    lane = lax.broadcasted_iota(jnp.int32, (1, 256), 1)
    inside = (lane >> 5) * 512 + (lane & 31)
    for side, audio_ref in enumerate(audio_refs):
        audio = audio_ref[...]
        on = core if side % 2 == 0 else 1 - core
        odd = par if side < 2 else 1 - par
        ids = (inside + (ylo * 8192 + on * 4096 + odd * 256 + (2 * x + yhi) * 32)).astype(F32)
        sims = lax.dot_general(unit_b, audio, (((1,), (1,)), ((), ())), preferred_element_type=F32)
        logits = cold * sims + offset
        hit = None
        for target in targets:
            same = target == ids
            hit = same if hit is None else hit | same
        weight = (jax.nn.sigmoid(logits) - jnp.where(hit, 1.0, 0.0)).astype(BF)
        term = jnp.dot(weight, audio, preferred_element_type=F32)
        total = term if total is None else total + term
    grad = cold * total
    unit = unit_ref[...]
    inner = jnp.sum(unit * grad, axis=1, keepdims=True)
    gp = ((grad - unit * inner) / mag_ref[:, :1]).astype(BF)
    gp = jnp.dot(gp, order_ref[...], preferred_element_type=F32).astype(BF)
    for h in range(2):
        for t in range(8):
            out_ref[2 * t + h] = gp[256 * h : 256 * (h + 1), 128 * t : 128 * (t + 1)]


def sum_kernel(g_ref, out_ref):
    total = g_ref[0].astype(F32)
    for s in range(1, g_ref.shape[0]):
        total = total + g_ref[s].astype(F32)
    out_ref[...] = total.astype(BF)


def weight_kernel(place_ref, mine_ref, other_ref, x_ref, keep_ref, give_ref):
    ylo = place_ref[1]
    lanes = pl.ds(pl.multiple_of(ylo * 640, 128), 640)
    part = None
    for gp_ref, half in ((mine_ref, ylo), (other_ref, 1 - ylo)):
        rows = x_ref[pl.ds(pl.multiple_of(half * 256, 256), 256), lanes]
        term = lax.dot_general(gp_ref[...], rows, (((0,), (0,)), ((), ())), preferred_element_type=F32)
        part = term if part is None else part + term
    first, second = (part[:, 320 * c : 320 * (c + 1)].reshape(16, 8, 320) for c in range(2))
    core = place_ref[2]
    keep_ref[...] = jnp.where(core == 0, first, second)
    give_ref[...] = jnp.where(core == 0, second, first).astype(BF)


def add_kernel(a_ref, b_ref, out_ref):
    out_ref[...] = (a_ref[...] + b_ref[...].astype(F32)).astype(BF)


def fetch(a):
    perm = [((i + 1) % 16, i) for i in range(16)] + [(16 + (i - 1) % 16, 16 + i) for i in range(16)]
    return lax.ppermute(a, ("core", *Z), perm)


def behind(a, *others):
    anywhere = pl.BlockSpec(memory_space=pl.ANY)
    return pl.pallas_call(
        lambda *refs: None,
        in_specs=[anywhere] * (1 + len(others)),
        out_specs=anywhere,
        out_shape=jax.ShapeDtypeStruct(a.shape, a.dtype),
        input_output_aliases={0: 0},
        compiler_params=pltpu.CompilerParams(vmem_limit_bytes=2**16),
    )(a, *others)


def swap(a, axis):
    return lax.ppermute(a, axis, [(0, 1), (1, 0)])


def local(frames, projector, sounds, matched, coldness, offset):
    ylo, core, zp, par, x, yhi = (lax.axis_index(a) for a in AXES)
    smem = pl.BlockSpec(memory_space=pltpu.SMEM)
    vmem = pl.BlockSpec(memory_space=pltpu.VMEM)

    place = jnp.stack([yhi, ylo, core, x, par]).astype(jnp.int32)

    wide = pl.pallas_call(
        spread_kernel,
        in_specs=[smem, pl.BlockSpec(memory_space=pltpu.HBM), pl.BlockSpec(memory_space=pltpu.HBM)],
        out_specs=pl.BlockSpec(memory_space=pltpu.HBM),
        out_shape=jax.ShapeDtypeStruct((8, 64, 1280 + PAD), BF),
        scratch_shapes=[pltpu.VMEM((64, 1280 + PAD), BF), pltpu.VMEM((5, 128), jnp.int32), pltpu.SemaphoreType.DMA((10,))],
        compiler_params=pltpu.CompilerParams(vmem_limit_bytes=4 * 2**20),
    )(core.reshape(1).astype(jnp.int32), pltpu.with_memory_space_constraint(frames, pltpu.HBM), pltpu.with_memory_space_constraint(matched.T, pltpu.HBM))
    rows = lax.all_to_all(wide, ("x", "yhi"), 0, 0, tiled=True)
    rows = rows.reshape(512, 1280 + PAD)

    even = lax.all_gather(sounds, "zp", axis=0, tiled=True)
    odd = fetch(even)
    far_even = swap(even, "core")
    units = pl.pallas_call(
        project_kernel,
        in_specs=[vmem] * 2,
        out_specs=[vmem] * 3,
        out_shape=[
            jax.ShapeDtypeStruct((512, 1024), F32),
            jax.ShapeDtypeStruct((512, 1024), BF),
            jax.ShapeDtypeStruct((512, 128), F32),
        ],
        compiler_params=PARAMS,
        cost_estimate=pl.CostEstimate(flops=2 * 512 * 1280 * 1024, bytes_accessed=9 * 2**20, transcendentals=0),
    )(rows, projector)
    odd = behind(odd, units[2], place)
    far_odd = swap(odd, "core")

    parts = pl.pallas_call(
        pair_kernel,
        in_specs=[smem] * 3 + [vmem] * 9,
        out_specs=vmem,
        out_shape=jax.ShapeDtypeStruct((16, 256, 128), BF),
        compiler_params=PARAMS,
        cost_estimate=pl.CostEstimate(flops=5 * 512 * 1024 * 1024, bytes_accessed=8 * 2**20, transcendentals=2**20),
    )(
        coldness,
        offset,
        place,
        rows,
        *units,
        column_order(),
        even,
        far_even,
        odd,
        far_odd,
    )

    terms = lax.all_to_all(parts, PLANE, 0, 0, tiled=True)
    mine = pl.pallas_call(
        sum_kernel, in_specs=[vmem], out_specs=vmem, out_shape=jax.ShapeDtypeStruct((256, 128), BF), compiler_params=PARAMS
    )(terms)
    keep, give = pl.pallas_call(
        weight_kernel,
        in_specs=[smem] + [vmem] * 3,
        out_specs=[vmem, vmem],
        out_shape=[jax.ShapeDtypeStruct((16, 8, 320), F32), jax.ShapeDtypeStruct((16, 8, 320), BF)],
        compiler_params=PARAMS,
    )(place, mine, swap(mine, "ylo"), rows)
    mine = pl.pallas_call(
        add_kernel,
        in_specs=[vmem, vmem],
        out_specs=vmem,
        out_shape=jax.ShapeDtypeStruct((16, 8, 320), BF),
        compiler_params=PARAMS,
    )(keep, swap(give, "core"))
    sums = lax.all_to_all(mine, Z, 0, 0, tiled=True)
    return jnp.sum(sums.astype(F32), axis=0).T


def solution(mesh):
    fine = Mesh(mesh.devices.reshape(SIZES), AXES)
    return jax.shard_map(
        local,
        mesh=fine,
        in_specs=(P(DP, None), P(), P(AXES, None), P(DP, None), P(), P()),
        out_specs=P(CHIP, DP),
        check_vma=False,
    )
```
